256 devices in a mesh: gx: 32 (over y_lo, z, core), gy: 8 (over x, y_hi).
Axes of the slice: x: 4, y: 4 (y_hi: 2, y_lo: 2; y = y_hi * 2 + y_lo), z: 8, core: 2. Of those that a mesh axis runs over, the one named last changes fastest.
Arguments:
- eigen_vecs: bfloat16 [2, 3, 4, 128, 128, 512], P(None, None, None, 'gx', 'gy'), may hold values from -6 to 6
- gauge_links: float32 [2, 2, 3, 3, 4, 128, 128], P(None, None, None, None, None, 'gx', 'gy'), may hold values from -4 to 4
- directions: int32 [4], replicated, may hold values from 0 to 3, each once
- spin_map: int32 [4], replicated, may hold values from 0 to 3, each once
- perambulator: bfloat16 [2, 2048, 2048], P(None, ('gx', 'gy')), may hold values from -0.125 to 0.125
Outputs:
- elementals: float32 [4, 2, 512, 512], P(None, None, 'gx')
- contracted: bfloat16 [4, 2, 2048, 2048], P(None, None, ('gx', 'gy'))
The draws below stay inside these ranges and needn't reach their ends.
Inputs may be any that keep to these rules, and one draw needn't show every extreme that they name: `directions`: a permutation of the four hops: 0 and 1 are forward hops along x and y, 2 and 3 backward hops along x and y. `spin_map`: a permutation of the four spins.
All inputs are finite; a program needn't handle non-finite values.
Results may differ from the reference program's by a relative error of at most 0.0058.
Values may be sent and summed in bfloat16 or wider, within the bound.
A program may use at most 128 MiB of HBM per device.

```python
import math
import jax
import jax.numpy as jnp
from jax import lax

NEV = 512
NDISP = 4
NZ = 4
NX = 128
NY = 128
PERAM = 2048


def level_of(rng, extent, pieces, low, top_value):
    def one(position, shards_of):
        draws = jax.random.uniform(jax.random.fold_in(jax.random.fold_in(rng, 6), position), (shards_of,), jnp.float32, low / len(pieces), top_value / len(pieces))
        return jnp.repeat(jnp.exp(draws), extent[position] // shards_of).reshape((-1,) + (1,) * (len(extent) - position - 1))

    loudness = one(*pieces[0])
    for cut in pieces[1:]:
        loudness = loudness * one(*cut)
    return loudness


def bell_draw(stream_key, dims, spread, most, split=(), kind=jnp.bfloat16):
    factor_of = level_of(stream_key, dims, split, -0.22, 0.18) if split else 1.0
    result = jax.random.normal(stream_key, dims, jnp.float32) * spread * factor_of
    return jnp.minimum(jnp.maximum(result, -most), most).astype(kind)


def setup_inputs(seed: int = 0) -> dict:
    key_list = jax.random.split(jax.random.key(seed), 6)
    return {
        "eigen_vecs": bell_draw(key_list[0], (2, 3, NZ, NX, NY, NEV), 1.0, 6.0, ((3, 32), (4, 8))),
        "gauge_links": bell_draw(key_list[1], (2, 2, 3, 3, NZ, NX, NY), 0.577, 4.0, ((5, 32), (6, 8)), jnp.float32),
        "directions": jax.random.permutation(key_list[2], 4).astype(jnp.int32),
        "spin_map": jax.random.permutation(key_list[3], 4).astype(jnp.int32),
        "perambulator": bell_draw(key_list[4], (2, PERAM, PERAM), PERAM ** -0.5, 0.125, ((1, 256),)),
    }


def colour_apply(gauge_link, colour_field, dagger):
    values = colour_field.astype(jnp.float32)
    rows_re = []
    rows_im = []
    for row in range(3):
        acc_re = jnp.zeros(values.shape[2:], jnp.float32)
        acc_im = jnp.zeros(values.shape[2:], jnp.float32)
        for column in range(3):
            if dagger:
                coef_re = gauge_link[0, column, row][..., None]
                coef_im = -gauge_link[1, column, row][..., None]
            else:
                coef_re = gauge_link[0, row, column][..., None]
                coef_im = gauge_link[1, row, column][..., None]
            acc_re = acc_re + coef_re * values[0, column] - coef_im * values[1, column]
            acc_im = acc_im + coef_re * values[1, column] + coef_im * values[0, column]
        rows_re.append(acc_re)
        rows_im.append(acc_im)
    return jnp.stack([jnp.stack(rows_re, 0), jnp.stack(rows_im, 0)], 0)

def gram_term(field, displaced):
    count = field.shape[-1]
    left_re = field[0].reshape(-1, count)
    left_im = field[1].reshape(-1, count)
    right_re = displaced[0].reshape(-1, count)
    right_im = displaced[1].reshape(-1, count)
    real = jnp.dot(left_re.T, right_re, preferred_element_type=jnp.float32) + jnp.dot(left_im.T, right_im, preferred_element_type=jnp.float32)
    imag = jnp.dot(left_re.T, right_im, preferred_element_type=jnp.float32) - jnp.dot(left_im.T, right_re, preferred_element_type=jnp.float32)
    return jnp.stack([real, imag], 0)

def displaced_plane(eigen_vecs, gauge_links, plane, heading):
    after = (plane + 1) % NX
    before = (plane - 1 + NX) % NX
    field_here = lax.dynamic_index_in_dim(eigen_vecs, plane, 3, keepdims=False)
    links_here = lax.dynamic_index_in_dim(gauge_links, plane, 5, keepdims=False)

    def forward_x():
        field_after = lax.dynamic_index_in_dim(eigen_vecs, after, 3, keepdims=False)
        return colour_apply(links_here[0], field_after, False).astype(jnp.bfloat16)

    def forward_y():
        return colour_apply(links_here[1], jnp.roll(field_here, -1, axis=3), False).astype(jnp.bfloat16)

    def backward_x():
        field_before = lax.dynamic_index_in_dim(eigen_vecs, before, 3, keepdims=False)
        links_before = lax.dynamic_index_in_dim(gauge_links, before, 5, keepdims=False)
        return colour_apply(links_before[0], field_before, True).astype(jnp.bfloat16)

    def backward_y():
        source_here = colour_apply(links_here[1], field_here, True).astype(jnp.bfloat16)
        return jnp.roll(source_here, 1, axis=3)
    return (field_here, lax.switch(heading, [forward_x, forward_y, backward_x, backward_y]))

def reference(eigen_vecs, gauge_links, directions, spin_map, perambulator):
    norm_factor = 1.0 / math.sqrt(3.0 * NX * NY * NZ)
    planes = jnp.arange(NX, dtype=jnp.int32)
    results = []
    for disp_index in range(NDISP):
        heading = directions[disp_index]

        def advance(running, plane):
            field_here, displaced = displaced_plane(eigen_vecs, gauge_links, plane, heading)
            return (running + gram_term(field_here, displaced), None)
        running, unused_out = lax.scan(advance, jnp.zeros((2, NEV, NEV), jnp.float32), planes)
        results.append(running * norm_factor)
    elementals = jnp.stack(results, 0)
    rounded = elementals.astype(jnp.bfloat16)
    onehot = (spin_map[:, None] == jnp.arange(4, dtype=jnp.int32)[None, :]).astype(jnp.float32)
    blocks = perambulator.reshape(2, PERAM, 4, NEV).astype(jnp.float32)
    chosen = jnp.einsum('prtn,st->prsn', blocks, onehot).astype(jnp.bfloat16)
    lhs_block = jnp.concatenate([chosen[0], chosen[1]], axis=-1).reshape(PERAM * 4, 2 * NEV)
    outputs = []
    for disp_index in range(NDISP):
        part_re = rounded[disp_index, 0]
        part_im = rounded[disp_index, 1]
        rhs_block = jnp.concatenate([jnp.concatenate([part_re, part_im], 1), jnp.concatenate([-part_im, part_re], 1)], 0)
        product = jnp.dot(lhs_block, rhs_block, preferred_element_type=jnp.float32)
        product = product.reshape(PERAM, 4, 2, NEV).transpose(2, 0, 1, 3).reshape(2, PERAM, PERAM)
        outputs.append(product.astype(jnp.bfloat16))
    return (elementals, jnp.stack(outputs, 0))
```

```python
import math

import jax
import jax.numpy as jnp
from jax import lax
from jax.experimental import pallas as pl
from jax.experimental.pallas import tpu as pltpu
from jax.sharding import PartitionSpec as P

MESH = pl.DeviceIdType.MESH
F32 = jnp.float32
BF16 = jnp.bfloat16
NX_RING, NY_RING, NZ_RING, CORES = 4, 4, 8, 2
LANES = 128


def device_at(core, x, y, z):
    return (((y % 2) * NZ_RING + z) * CORES + core, x * 2 + y // 2)


def reduce_kernel(norm, ev, links, out, vt, right, face_f, face, halo_y, halo_yf, halo_x, send0, own, recv0,
                  send1, recv1, own2, send2, recv2, own3, send3, recv3,
                  halo_send, halo_recv, core_send, core_recv, ring_send, ring_recv, z_send, z_recv):
    gx, gy = lax.axis_index("gx"), lax.axis_index("gy")
    core, z = gx % 2, (gx // 2) % NZ_RING
    x, y = gy // 2, (gy % 2) * 2 + gx // (2 * NZ_RING)
    n_gx, n_gy = 2 * 2 * NZ_RING, 2 * NX_RING
    sibling = device_at(1 - core, x, y, z)

    def at_x(d):
        return device_at(core, (x + d) % NX_RING, y, z)

    def at_y(d):
        return device_at(core, x, (y + d) % NY_RING, z)

    def at_z(d):
        return device_at(core, x, y, (z + d) % NZ_RING)

    before_x, after_x = ((gx + n_gx - 1) % n_gx, gy), ((gx + 1) % n_gx, gy)
    before_y, after_y = (gx, (gy + n_gy - 1) % n_gy), (gx, (gy + 1) % n_gy)

    barrier = pltpu.get_barrier_semaphore()
    peers = [before_x, after_x, before_y, after_y, sibling]
    peers += [at_x(d) for d in range(1, NX_RING)]
    peers += [at_y(d) for d in range(1, NY_RING)]
    peers += [at_z(d) for d in range(1, NZ_RING)]
    for peer in peers:
        pl.semaphore_signal(barrier, inc=1, device_id=peer, device_id_type=MESH)

    planes = ev.shape[2]

    def take_face(s, carry):
        for p in range(2):
            for c in range(3):
                face_f[pl.ds((p * 3 + c) * planes + s, 1), :] = ev[p, c, s].astype(F32)[0:1, :]
        return carry

    lax.fori_loop(0, planes, take_face, 0)
    face[...] = face_f[...].astype(BF16)
    pl.semaphore_wait(barrier, len(peers))

    started = []

    def send(src, dst, s_sem, r_sem, to):
        copy = pltpu.make_async_remote_copy(
            src_ref=src, dst_ref=dst, send_sem=s_sem, recv_sem=r_sem, device_id=to, device_id_type=MESH
        )
        copy.start()
        started.append(copy)
        return copy

    copy_y = send(face, halo_y, halo_send.at[0], halo_recv.at[0], before_y)
    nz = planes // 4
    copies_x = []
    for zz in range(nz):
        copies_x.append(
            send(ev.at[:, :, zz * 4], halo_x.at[:, :, zz], halo_send.at[1 + zz], halo_recv.at[1 + zz], before_x)
        )

    vt[...] = ev[...].reshape(-1, ev.shape[-1]).T

    def colour(h, s, source):
        cols = links[pl.ds((1 - h) * 18 * planes + s, 18, stride=planes), :].T
        coef = [jnp.broadcast_to(cols[:, i : i + 1], (16, LANES)) for i in range(18)]
        for lane in range(ev.shape[-1] // LANES):
            at = slice(lane * LANES, (lane + 1) * LANES)
            v = [[source(p, c, at) for c in range(3)] for p in range(2)]
            for a in range(3):
                re = im = None
                for b in range(3):
                    u_re, u_im = coef[a * 3 + b], coef[9 + a * 3 + b]
                    t_re = u_re * v[0][b] - u_im * v[1][b]
                    t_im = u_re * v[1][b] + u_im * v[0][b]
                    re = t_re if re is None else re + t_re
                    im = t_im if im is None else im + t_im
                re, im = re.astype(BF16), im.astype(BF16)
                right[h, 0, 0, a, s, :, at] = re
                right[h, 0, 1, a, s, :, at] = im
                right[h, 1, 0, a, s, :, at] = im
                right[h, 1, 1, a, s, :, at] = -re

    def gram(h, q):
        lhs = vt[...]
        wide = 2 * LANES
        for j in range(ev.shape[-1] // wide):
            rhs = right[h, q, :, :, :, :, j * wide : (j + 1) * wide].reshape(-1, wide)
            yield j, jnp.dot(lhs, rhs, preferred_element_type=F32) * norm

    rows = ev.shape[-1]

    def gram_other(h):
        for j, value in gram(h, 1 - core):
            for half in range(2):
                send0[h, (2 * j + half) * rows : (2 * j + half + 1) * rows, :] = value[
                    :, half * LANES : (half + 1) * LANES
                ].astype(BF16)
        return send(send0.at[h], recv0.at[h], core_send.at[h, 0], core_recv.at[h, 0], sibling)

    def gram_own(h):
        for j, value in gram(h, core):
            for half in range(2):
                own[h, (2 * j + half) * rows : (2 * j + half + 1) * rows, :] = value[
                    :, half * LANES : (half + 1) * LANES
                ]

    first = ((x, at_x), (y, at_y))
    second = ((y, at_y), (x, at_x))
    len1, len2, len3 = own.shape[1] // 4, own.shape[1] // 16, own.shape[1] // 128

    def start1(h, copy):
        copy.wait_recv()
        total = own[h] + recv0[h].astype(F32)
        own[h] = total
        send1[h] = total.astype(BF16)
        place, at = first[h]
        return [
            send(send1.at[h, pl.ds((place + d) % 4 * len1, len1)], recv1.at[h, d - 1],
                 ring_send.at[h, 0, d - 1], ring_recv.at[h, 0, d - 1], at(d))
            for d in range(1, 4)
        ]

    def start2(h, copies):
        total = own[h, pl.ds(first[h][0] * len1, len1)]
        for d, copy in enumerate(copies):
            copy.wait_recv()
            total = total + recv1[h, d].astype(F32)
        own2[h] = total
        send2[h] = total.astype(BF16)
        place, at = second[h]
        return [
            send(send2.at[h, pl.ds((place + d) % 4 * len2, len2)], recv2.at[h, d - 1],
                 ring_send.at[h, 1, d - 1], ring_recv.at[h, 1, d - 1], at(d))
            for d in range(1, 4)
        ]

    def start3(h, copies):
        total = own2[h, pl.ds(second[h][0] * len2, len2)]
        for d, copy in enumerate(copies):
            copy.wait_recv()
            total = total + recv2[h, d].astype(F32)
        own3[h] = total
        send3[h] = total.astype(BF16)
        return [
            send(send3.at[h, pl.ds((z + d) % NZ_RING * len3, len3)], recv3.at[h, d - 1],
                 z_send.at[h, 0, d - 1], z_recv.at[h, 0, d - 1], at_z(d))
            for d in range(1, NZ_RING)
        ]

    def base(h):
        b0 = core * own.shape[1]
        b1 = b0 + first[h][0] * len1
        b2 = b1 + second[h][0] * len2
        return b0, b1, b2, b2 + z * len3

    def gather3(h, copies):
        total = own3[h, pl.ds(z * len3, len3)]
        for d, copy in enumerate(copies):
            copy.wait_recv()
            total = total + recv3[h, d].astype(F32)
        place = pl.ds(base(h)[3], len3)
        out[h, place] = total.astype(BF16)
        return [
            send(out.at[h, place], out.at[h, place], z_send.at[h, 1, d - 1], z_recv.at[h, 1, d - 1], at_z(d))
            for d in range(1, NZ_RING)
        ]

    def gather2(h, copies):
        for copy in copies:
            copy.wait_recv()
        place = pl.ds(base(h)[2], len2)
        at = second[h][1]
        return [
            send(out.at[h, place], out.at[h, place], ring_send.at[h, 2, d - 1], ring_recv.at[h, 2, d - 1], at(d))
            for d in range(1, 4)
        ]

    def to_sibling(h, d, place):
        return send(out.at[h, place], out.at[h, place], core_send.at[h, 1 + d], core_recv.at[h, 1 + d], sibling)

    def gather1(h, copies):
        for copy in copies:
            copy.wait_recv()
        place = pl.ds(base(h)[1], len1)
        at = first[h][1]
        ring = [
            send(out.at[h, place], out.at[h, place], ring_send.at[h, 3, d - 1], ring_recv.at[h, 3, d - 1], at(d))
            for d in range(1, 4)
        ]
        return ring, [to_sibling(h, 0, place)]

    def gather0(h, both):
        ring, across = both
        for d in (1, 3, 2):
            ring[d - 1].wait_recv()
            place = pl.ds(base(h)[0] + (first[h][0] + 4 - d) % 4 * len1, len1)
            across.append(to_sibling(h, d, place))
        return across

    def hop_x_inner(zz, carry):
        for xx in range(3):
            s = zz * 4 + xx
            colour(1, s, lambda p, c, at: ev[p, c, s + 1, :, at].astype(F32))
        return carry

    def hop_x_last(zz, carry):
        colour(1, zz * 4 + 3, lambda p, c, at: halo_x[p, c, zz, :, at].astype(F32))
        return carry

    def hop_y(s, carry):
        last = lax.broadcasted_iota(jnp.int32, (16, LANES), 0) == 15
        edges = [halo_yf[j, pl.ds(s, 6, stride=planes), :] for j in range(halo_yf.shape[0])]

        def source(p, c, at):
            value = pltpu.roll(ev[p, c, s, :, at].astype(F32), 15, 0)
            edge = edges[at.start // LANES][p * 3 + c : p * 3 + c + 1, :]
            return jnp.where(last, jnp.broadcast_to(edge, value.shape), value)

        colour(0, s, source)
        return carry

    lax.fori_loop(0, nz, hop_x_inner, 0)
    copy_y.wait_recv()
    for j in range(halo_yf.shape[0]):
        halo_yf[j] = halo_y[:, j * LANES : (j + 1) * LANES].astype(F32)
    lax.fori_loop(0, planes, hop_y, 0)
    a = gram_other(0)
    gram_own(0)
    a = start1(0, a)
    for copy in copies_x:
        copy.wait_recv()
    lax.fori_loop(0, nz, hop_x_last, 0)
    b = gram_other(1)
    a = start2(0, a)
    gram_own(1)
    b = start1(1, b)
    a = start3(0, a)
    a = gather3(0, a)
    b = start2(1, b)
    a = gather2(0, a)
    b = start3(1, b)
    a = gather1(0, a)
    b = gather3(1, b)
    a = gather0(0, a)
    b = gather2(1, b)
    b = gather1(1, b)
    b = gather0(1, b)
    for copy in a + b:
        copy.wait_recv()
    for copy in started:
        copy.wait_send()


def contract_kernel(directions, spins, g, peram, elementals, contracted, products):
    gx = lax.axis_index("gx")
    vecs = peram.shape[-1] // 4
    rows = peram.shape[1]
    own_rows = elementals.shape[2]
    pieces = [peram[p].astype(F32)[:, t * vecs : (t + 1) * vecs] for p in range(2) for t in range(4)]
    pick = lax.broadcasted_iota(jnp.int32, (own_rows, vecs), 1) == gx * own_rows + lax.broadcasted_iota(
        jnp.int32, (own_rows, vecs), 0
    )
    lhs = jnp.concatenate(pieces + [jnp.where(pick, 1.0, 0.0)], axis=0).astype(BF16)
    m = 4 * rows
    for h in range(2):
        parts = []
        for q in range(2):
            blocks = [g[h, (q * 4 + j) * vecs : (q * 4 + j + 1) * vecs, :] for j in range(4)]
            parts.append(jnp.concatenate(blocks, axis=1))
        re = jnp.dot(lhs, parts[0], preferred_element_type=F32)
        im = jnp.dot(lhs, parts[1], preferred_element_type=F32)
        products[h, 0] = jnp.concatenate([re[:m] - im[m : 2 * m], re[2 * m :]], 0)
        products[h, 1] = jnp.concatenate([im[:m] + re[m : 2 * m], im[2 * m :]], 0)
        over = (((1,), (1,)), ((), ()))
        re = lax.dot_general(lhs, parts[0], over, preferred_element_type=F32)
        im = lax.dot_general(lhs, parts[1], over, preferred_element_type=F32)
        products[2 + h, 0] = jnp.concatenate([re[:m] + im[m : 2 * m], re[2 * m :]], 0)
        products[2 + h, 1] = jnp.concatenate([re[m : 2 * m] - im[:m], -im[2 * m :]], 0)
    for k in range(4):
        which = jnp.where(directions[k] % 2 == 0, directions[k] + 1, directions[k] - 1)
        for q in range(2):
            elementals[k, q] = products[which, q, m : m + own_rows, :]
            for u in range(4):
                row = pl.multiple_of(spins[u] * rows, rows)
                contracted[k, q, :, u * vecs : (u + 1) * vecs] = products[which, q, pl.ds(row, rows), :].astype(BF16)


def local(eigen_vecs, gauge_links, directions, spin_map, perambulator):
    reim, colours, nz, nx, ny, vecs = eigen_vecs.shape
    sites = nz * nx * ny * lax.axis_size("gx") * lax.axis_size("gy")
    norm = 1.0 / math.sqrt(3.0 * sites)
    planes = nz * nx
    ev = eigen_vecs.reshape(reim, colours, planes, ny, vecs)
    links = gauge_links.reshape(-1, ny)
    half = vecs * vecs // LANES
    vmem = pl.BlockSpec(memory_space=pltpu.VMEM)
    faces = reim * colours * planes
    g = pl.pallas_call(
        lambda *refs: reduce_kernel(norm, *refs),
        out_shape=jax.ShapeDtypeStruct((2, 2 * half, LANES), BF16),
        in_specs=[vmem, vmem],
        out_specs=vmem,
        scratch_shapes=[
            pltpu.VMEM((vecs, reim * colours * planes * ny), BF16),
            pltpu.VMEM((2, 2, reim, colours, planes, ny, vecs), BF16),
            pltpu.VMEM((faces, vecs), F32),
            pltpu.VMEM((faces, vecs), BF16),
            pltpu.VMEM((faces, vecs), BF16),
            pltpu.VMEM((vecs // LANES, faces, LANES), F32),
            pltpu.VMEM((reim, colours, nz, ny, vecs), BF16),
            pltpu.VMEM((2, half, LANES), BF16),
            pltpu.VMEM((2, half, LANES), F32),
            pltpu.VMEM((2, half, LANES), BF16),
            pltpu.VMEM((2, half, LANES), BF16),
            pltpu.VMEM((2, 3, half // 4, LANES), BF16),
            pltpu.VMEM((2, half // 4, LANES), F32),
            pltpu.VMEM((2, half // 4, LANES), BF16),
            pltpu.VMEM((2, 3, half // 16, LANES), BF16),
            pltpu.VMEM((2, half // 16, LANES), F32),
            pltpu.VMEM((2, half // 16, LANES), BF16),
            pltpu.VMEM((2, NZ_RING - 1, half // 128, LANES), BF16),
            pltpu.SemaphoreType.DMA((1 + nz,)),
            pltpu.SemaphoreType.DMA((1 + nz,)),
            pltpu.SemaphoreType.DMA((2, 5)),
            pltpu.SemaphoreType.DMA((2, 5)),
            pltpu.SemaphoreType.DMA((2, 4, 3)),
            pltpu.SemaphoreType.DMA((2, 4, 3)),
            pltpu.SemaphoreType.DMA((2, 2, NZ_RING - 1)),
            pltpu.SemaphoreType.DMA((2, 2, NZ_RING - 1)),
        ],
        compiler_params=pltpu.CompilerParams(
            collective_id=0, has_side_effects=True, vmem_limit_bytes=48 * 2**20
        ),
        name="reduce",
    )(ev, links)
    rows = perambulator.shape[1]
    own_rows = vecs // lax.axis_size("gx")
    smem = pl.BlockSpec(memory_space=pltpu.SMEM)
    return pl.pallas_call(
        contract_kernel,
        out_shape=(
            jax.ShapeDtypeStruct((4, 2, own_rows, vecs), F32),
            jax.ShapeDtypeStruct((4, 2, rows, 4 * vecs), BF16),
        ),
        in_specs=[smem, smem, vmem, vmem],
        out_specs=(vmem, vmem),
        scratch_shapes=[pltpu.VMEM((4, 2, 4 * rows + own_rows, vecs), F32)],
        compiler_params=pltpu.CompilerParams(vmem_limit_bytes=32 * 2**20),
        name="contract",
    )(directions, spin_map, g, perambulator)


def solution(mesh):
    in_specs = (
        P(None, None, None, "gx", "gy", None),
        P(None, None, None, None, None, "gx", "gy"),
        P(),
        P(),
        P(None, ("gx", "gy"), None),
    )
    out_specs = (P(None, None, "gx", None), P(None, None, ("gx", "gy"), None))
    return jax.shard_map(local, mesh=mesh, in_specs=in_specs, out_specs=out_specs, check_vma=False)
```

```python
import math

import jax
import jax.numpy as jnp
from jax import lax
from jax.experimental import pallas as pl
from jax.experimental.pallas import tpu as pltpu
from jax.sharding import PartitionSpec as P

MESH = pl.DeviceIdType.MESH
F32 = jnp.float32
BF16 = jnp.bfloat16
NX_RING, NY_RING, NZ_RING, CORES = 4, 4, 8, 2
LANES = 128


def device_at(core, x, y, z):
    return (((y % 2) * NZ_RING + z) * CORES + core, x * 2 + y // 2)


def reduce_kernel(norm, ev_in, links_in, out, ev, links, vt, right, face_f, face, halo_y, halo_yf, halo_x, send0, own, recv0,
                  send1, recv1, own2, send2, recv2, own3, send3, recv3, done3,
                  load, halo_send, halo_recv, core_send, core_recv, ring_send, ring_recv, z_send, z_recv):
    gx, gy = lax.axis_index("gx"), lax.axis_index("gy")
    core, z = gx % 2, (gx // 2) % NZ_RING
    x, y = gy // 2, (gy % 2) * 2 + gx // (2 * NZ_RING)
    n_gx, n_gy = 2 * 2 * NZ_RING, 2 * NX_RING
    sibling = device_at(1 - core, x, y, z)

    def at_x(d):
        return device_at(core, (x + d) % NX_RING, y, z)

    def at_y(d):
        return device_at(core, x, (y + d) % NY_RING, z)

    def at_z(d):
        return device_at(core, x, y, (z + d) % NZ_RING)

    before_x, after_x = ((gx + n_gx - 1) % n_gx, gy), ((gx + 1) % n_gx, gy)
    before_y, after_y = (gx, (gy + n_gy - 1) % n_gy), (gx, (gy + 1) % n_gy)

    loads = [pltpu.make_async_copy(ev_in, ev, load.at[0]), pltpu.make_async_copy(links_in, links, load.at[1])]
    for copy in loads:
        copy.start()
    barrier = pltpu.get_barrier_semaphore()
    peers = [before_x, after_x, before_y, after_y, sibling]
    peers += [at_x(d) for d in range(1, NX_RING)]
    peers += [at_y(d) for d in range(1, NY_RING)]
    peers += [at_z(d) for d in range(1, NZ_RING)]
    for peer in peers:
        pl.semaphore_signal(barrier, inc=1, device_id=peer, device_id_type=MESH)

    planes = ev.shape[2]

    def take_face(s, carry):
        for p in range(2):
            for c in range(3):
                face_f[pl.ds((p * 3 + c) * planes + s, 1), :] = ev[p, c, s].astype(F32)[0:1, :]
        return carry

    loads[0].wait()
    lax.fori_loop(0, planes, take_face, 0)
    face[...] = face_f[...].astype(BF16)
    pl.semaphore_wait(barrier, len(peers))

    started = []

    def send(src, dst, s_sem, r_sem, to):
        copy = pltpu.make_async_remote_copy(
            src_ref=src, dst_ref=dst, send_sem=s_sem, recv_sem=r_sem, device_id=to, device_id_type=MESH
        )
        copy.start()
        started.append(copy)
        return copy

    copy_y = send(face, halo_y, halo_send.at[0], halo_recv.at[0], before_y)
    nz = planes // 4
    copies_x = []
    for zz in range(nz):
        copies_x.append(
            send(ev_in.at[:, :, zz * 4], halo_x.at[:, :, zz], halo_send.at[1 + zz], halo_recv.at[1 + zz], before_x)
        )

    vt[...] = ev[...].reshape(-1, ev.shape[-1]).T

    def colour(h, s, source):
        cols = links[pl.ds((1 - h) * 18 * planes + s, 18, stride=planes), :].T
        coef = [jnp.broadcast_to(cols[:, i : i + 1], (16, LANES)) for i in range(18)]
        for lane in range(ev.shape[-1] // LANES):
            at = slice(lane * LANES, (lane + 1) * LANES)
            v = [[source(p, c, at) for c in range(3)] for p in range(2)]
            for a in range(3):
                re = im = None
                for b in range(3):
                    u_re, u_im = coef[a * 3 + b], coef[9 + a * 3 + b]
                    t_re = u_re * v[0][b] - u_im * v[1][b]
                    t_im = u_re * v[1][b] + u_im * v[0][b]
                    re = t_re if re is None else re + t_re
                    im = t_im if im is None else im + t_im
                re, im = re.astype(BF16), im.astype(BF16)
                right[h, 0, 0, a, s, :, at] = re
                right[h, 0, 1, a, s, :, at] = im
                right[h, 1, 0, a, s, :, at] = im
                right[h, 1, 1, a, s, :, at] = -re

    def gram(h, q):
        lhs = vt[...]
        wide = 2 * LANES
        for j in range(ev.shape[-1] // wide):
            rhs = right[h, q, :, :, :, :, j * wide : (j + 1) * wide].reshape(-1, wide)
            yield j, jnp.dot(lhs, rhs, preferred_element_type=F32) * norm

    rows = ev.shape[-1]

    def gram_other(h):
        for j, value in gram(h, 1 - core):
            for half in range(2):
                send0[h, (2 * j + half) * rows : (2 * j + half + 1) * rows, :] = value[
                    :, half * LANES : (half + 1) * LANES
                ].astype(BF16)
        return send(send0.at[h], recv0.at[h], core_send.at[h, 0], core_recv.at[h, 0], sibling)

    def gram_own(h):
        for j, value in gram(h, core):
            for half in range(2):
                own[h, (2 * j + half) * rows : (2 * j + half + 1) * rows, :] = value[
                    :, half * LANES : (half + 1) * LANES
                ]

    first = ((x, at_x), (y, at_y))
    second = ((y, at_y), (x, at_x))
    half = own.shape[1]
    part, len1, len2, len3 = half // 2, half // 8, half // 32, half // 256

    def start1(h, copy):
        copy.wait_recv()
        total = own[h] + recv0[h].astype(F32)
        own[h] = total
        send1[h] = total.astype(BF16)
        return [
            [
                send(send1.at[h, pl.ds(s * part + (first[s][0] + d) % 4 * len1, len1)], recv1.at[h, s, d - 1],
                     ring_send.at[h, 0, s, d - 1], ring_recv.at[h, 0, s, d - 1], first[s][1](d))
                for d in range(1, 4)
            ]
            for s in range(2)
        ]

    def start2(h, copies):
        result = []
        for s in range(2):
            total = own[h, pl.ds(s * part + first[s][0] * len1, len1)]
            for d, copy in enumerate(copies[s]):
                copy.wait_recv()
                total = total + recv1[h, s, d].astype(F32)
            own2[h, s] = total
            send2[h, s] = total.astype(BF16)
            place, at = second[s]
            result.append([
                send(send2.at[h, s, pl.ds((place + d) % 4 * len2, len2)], recv2.at[h, s, d - 1],
                     ring_send.at[h, 1, s, d - 1], ring_recv.at[h, 1, s, d - 1], at(d))
                for d in range(1, 4)
            ])
        return result

    def start3(h, copies):
        totals = []
        for s in range(2):
            total = own2[h, s, pl.ds(second[s][0] * len2, len2)]
            for d, copy in enumerate(copies[s]):
                copy.wait_recv()
                total = total + recv2[h, s, d].astype(F32)
            totals.append(total)
        total = jnp.concatenate(
            [totals[s][i * len3 : (i + 1) * len3] for i in range(NZ_RING) for s in range(2)], axis=0
        )
        own3[h] = total
        send3[h] = total.astype(BF16)
        return [
            send(send3.at[h, pl.ds((z + d) % NZ_RING * 2 * len3, 2 * len3)], recv3.at[h, d - 1],
                 z_send.at[h, 0, d - 1], z_recv.at[h, 0, d - 1], at_z(d))
            for d in range(1, NZ_RING)
        ]

    def base(s):
        b0 = core * half + s * part
        b1 = b0 + first[s][0] * len1
        return b0, b1, b1 + second[s][0] * len2

    def gather3(h, copies):
        place = pl.ds(z * 2 * len3, 2 * len3)
        total = own3[h, place]
        for d, copy in enumerate(copies):
            copy.wait_recv()
            total = total + recv3[h, d].astype(F32)
        done3[h, place] = total.astype(BF16)
        return [
            send(done3.at[h, place], done3.at[h, place], z_send.at[h, 1, d - 1], z_recv.at[h, 1, d - 1], at_z(d))
            for d in range(1, NZ_RING)
        ]

    def gather2(h, copies):
        for copy in copies:
            copy.wait_recv()
        value = done3[h].astype(F32)
        result = []
        for s in range(2):
            place = pl.ds(base(s)[2], len2)
            out[h, place] = jnp.concatenate(
                [value[(2 * i + s) * len3 : (2 * i + s + 1) * len3] for i in range(NZ_RING)], axis=0
            ).astype(BF16)
            result += [
                send(out.at[h, place], out.at[h, place], ring_send.at[h, 2, s, d - 1], ring_recv.at[h, 2, s, d - 1],
                     second[s][1](d))
                for d in range(1, 4)
            ]
        return result

    def to_sibling(h, s, d, place):
        return send(out.at[h, place], out.at[h, place], core_send.at[h, 1 + 4 * s + d], core_recv.at[h, 1 + 4 * s + d],
                    sibling)

    def gather1(h, copies):
        for copy in copies:
            copy.wait_recv()
        rings, across = [], []
        for s in range(2):
            place = pl.ds(base(s)[1], len1)
            rings.append([
                send(out.at[h, place], out.at[h, place], ring_send.at[h, 3, s, d - 1], ring_recv.at[h, 3, s, d - 1],
                     first[s][1](d))
                for d in range(1, 4)
            ])
            across.append(to_sibling(h, s, 0, place))
        return rings, across

    def gather0(h, both):
        rings, across = both
        for d in (1, 3, 2):
            for s in range(2):
                rings[s][d - 1].wait_recv()
                place = pl.ds(base(s)[0] + (first[s][0] + 4 - d) % 4 * len1, len1)
                across.append(to_sibling(h, s, d, place))
        return across

    def hop_x_inner(zz, carry):
        for xx in range(3):
            s = zz * 4 + xx
            colour(1, s, lambda p, c, at: ev[p, c, s + 1, :, at].astype(F32))
        return carry

    def hop_x_last(zz, carry):
        colour(1, zz * 4 + 3, lambda p, c, at: halo_x[p, c, zz, :, at].astype(F32))
        return carry

    def hop_y(s, carry):
        last = lax.broadcasted_iota(jnp.int32, (16, LANES), 0) == 15
        edges = [halo_yf[j, pl.ds(s, 6, stride=planes), :] for j in range(halo_yf.shape[0])]

        def source(p, c, at):
            value = pltpu.roll(ev[p, c, s, :, at].astype(F32), 15, 0)
            edge = edges[at.start // LANES][p * 3 + c : p * 3 + c + 1, :]
            return jnp.where(last, jnp.broadcast_to(edge, value.shape), value)

        colour(0, s, source)
        return carry

    loads[1].wait()
    lax.fori_loop(0, nz, hop_x_inner, 0)
    copy_y.wait_recv()
    for j in range(halo_yf.shape[0]):
        halo_yf[j] = halo_y[:, j * LANES : (j + 1) * LANES].astype(F32)
    lax.fori_loop(0, planes, hop_y, 0)
    a = gram_other(0)
    gram_own(0)
    a = start1(0, a)
    for copy in copies_x:
        copy.wait_recv()
    lax.fori_loop(0, nz, hop_x_last, 0)
    b = gram_other(1)
    gram_own(1)
    b = start1(1, b)
    for step in (start2, start3, gather3, gather2, gather1, gather0):
        a = step(0, a)
        b = step(1, b)
    for copy in a + b:
        copy.wait_recv()
    for copy in started:
        copy.wait_send()


def contract_kernel(directions, spins, g, peram, elementals, contracted, products):
    gx = lax.axis_index("gx")
    vecs = peram.shape[-1] // 4
    rows = peram.shape[1]
    own_rows = elementals.shape[2]
    pieces = [peram[p].astype(F32)[:, t * vecs : (t + 1) * vecs] for p in range(2) for t in range(4)]
    pick = lax.broadcasted_iota(jnp.int32, (own_rows, vecs), 1) == gx * own_rows + lax.broadcasted_iota(
        jnp.int32, (own_rows, vecs), 0
    )
    lhs = jnp.concatenate(pieces + [jnp.where(pick, 1.0, 0.0)], axis=0).astype(BF16)
    m = 4 * rows
    for h in range(2):
        parts = []
        for q in range(2):
            blocks = [g[h, (q * 4 + j) * vecs : (q * 4 + j + 1) * vecs, :] for j in range(4)]
            parts.append(jnp.concatenate(blocks, axis=1))
        re = jnp.dot(lhs, parts[0], preferred_element_type=F32)
        im = jnp.dot(lhs, parts[1], preferred_element_type=F32)
        products[h, 0] = jnp.concatenate([re[:m] - im[m : 2 * m], re[2 * m :]], 0)
        products[h, 1] = jnp.concatenate([im[:m] + re[m : 2 * m], im[2 * m :]], 0)
        over = (((1,), (1,)), ((), ()))
        re = lax.dot_general(lhs, parts[0], over, preferred_element_type=F32)
        im = lax.dot_general(lhs, parts[1], over, preferred_element_type=F32)
        products[2 + h, 0] = jnp.concatenate([re[:m] + im[m : 2 * m], re[2 * m :]], 0)
        products[2 + h, 1] = jnp.concatenate([re[m : 2 * m] - im[:m], -im[2 * m :]], 0)
    for k in range(4):
        which = jnp.where(directions[k] % 2 == 0, directions[k] + 1, directions[k] - 1)
        for q in range(2):
            elementals[k, q] = products[which, q, m : m + own_rows, :]
            for u in range(4):
                row = pl.multiple_of(spins[u] * rows, rows)
                contracted[k, q, :, u * vecs : (u + 1) * vecs] = products[which, q, pl.ds(row, rows), :].astype(BF16)


def local(eigen_vecs, gauge_links, directions, spin_map, perambulator):
    reim, colours, nz, nx, ny, vecs = eigen_vecs.shape
    sites = nz * nx * ny * lax.axis_size("gx") * lax.axis_size("gy")
    norm = 1.0 / math.sqrt(3.0 * sites)
    planes = nz * nx
    ev = eigen_vecs.reshape(reim, colours, planes, ny, vecs)
    links = gauge_links.reshape(-1, ny)
    half = vecs * vecs // LANES
    vmem = pl.BlockSpec(memory_space=pltpu.VMEM)
    faces = reim * colours * planes
    g = pl.pallas_call(
        lambda *refs: reduce_kernel(norm, *refs),
        out_shape=jax.ShapeDtypeStruct((2, 2 * half, LANES), BF16),
        in_specs=[pl.BlockSpec(memory_space=pltpu.HBM)] * 2,
        out_specs=vmem,
        scratch_shapes=[
            pltpu.VMEM(ev.shape, BF16),
            pltpu.VMEM(links.shape, F32),
            pltpu.VMEM((vecs, reim * colours * planes * ny), BF16),
            pltpu.VMEM((2, 2, reim, colours, planes, ny, vecs), BF16),
            pltpu.VMEM((faces, vecs), F32),
            pltpu.VMEM((faces, vecs), BF16),
            pltpu.VMEM((faces, vecs), BF16),
            pltpu.VMEM((vecs // LANES, faces, LANES), F32),
            pltpu.VMEM((reim, colours, nz, ny, vecs), BF16),
            pltpu.VMEM((2, half, LANES), BF16),
            pltpu.VMEM((2, half, LANES), F32),
            pltpu.VMEM((2, half, LANES), BF16),
            pltpu.VMEM((2, half, LANES), BF16),
            pltpu.VMEM((2, 2, 3, half // 8, LANES), BF16),
            pltpu.VMEM((2, 2, half // 8, LANES), F32),
            pltpu.VMEM((2, 2, half // 8, LANES), BF16),
            pltpu.VMEM((2, 2, 3, half // 32, LANES), BF16),
            pltpu.VMEM((2, half // 16, LANES), F32),
            pltpu.VMEM((2, half // 16, LANES), BF16),
            pltpu.VMEM((2, NZ_RING - 1, half // 128, LANES), BF16),
            pltpu.VMEM((2, half // 16, LANES), BF16),
            pltpu.SemaphoreType.DMA((2,)),
            pltpu.SemaphoreType.DMA((1 + nz,)),
            pltpu.SemaphoreType.DMA((1 + nz,)),
            pltpu.SemaphoreType.DMA((2, 9)),
            pltpu.SemaphoreType.DMA((2, 9)),
            pltpu.SemaphoreType.DMA((2, 4, 2, 3)),
            pltpu.SemaphoreType.DMA((2, 4, 2, 3)),
            pltpu.SemaphoreType.DMA((2, 2, NZ_RING - 1)),
            pltpu.SemaphoreType.DMA((2, 2, NZ_RING - 1)),
        ],
        compiler_params=pltpu.CompilerParams(
            collective_id=0, has_side_effects=True, vmem_limit_bytes=48 * 2**20
        ),
        name="reduce",
    )(ev, links)
    rows = perambulator.shape[1]
    own_rows = vecs // lax.axis_size("gx")
    smem = pl.BlockSpec(memory_space=pltpu.SMEM)
    return pl.pallas_call(
        contract_kernel,
        out_shape=(
            jax.ShapeDtypeStruct((4, 2, own_rows, vecs), F32),
            jax.ShapeDtypeStruct((4, 2, rows, 4 * vecs), BF16),
        ),
        in_specs=[smem, smem, vmem, vmem],
        out_specs=(vmem, vmem),
        scratch_shapes=[pltpu.VMEM((4, 2, 4 * rows + own_rows, vecs), F32)],
        compiler_params=pltpu.CompilerParams(vmem_limit_bytes=32 * 2**20),
        name="contract",
    )(directions, spin_map, g, perambulator)


def solution(mesh):
    in_specs = (
        P(None, None, None, "gx", "gy", None),
        P(None, None, None, None, None, "gx", "gy"),
        P(),
        P(),
        P(None, ("gx", "gy"), None),
    )
    out_specs = (P(None, None, "gx", None), P(None, None, ("gx", "gy"), None))
    return jax.shard_map(local, mesh=mesh, in_specs=in_specs, out_specs=out_specs, check_vma=False)
```

```python
import math

import jax
import jax.numpy as jnp
from jax import lax
from jax.experimental import pallas as pl
from jax.experimental.pallas import tpu as pltpu
from jax.sharding import PartitionSpec as P

MESH = pl.DeviceIdType.MESH
F32 = jnp.float32
BF16 = jnp.bfloat16
NX_RING, NY_RING, NZ_RING, CORES = 4, 4, 8, 2
LANES = 128


def device_at(core, x, y, z):
    return (((y % 2) * NZ_RING + z) * CORES + core, x * 2 + y // 2)


def reduce_kernel(norm, ev_in, links_in, out, ev, links, vt, right, face_f, face, halo_y, halo_x, send0, own, other, recv0,
                  send1, recv1, own2, send2, recv2, own3, send3, recv3, done3,
                  load, halo_send, halo_recv, core_send, core_recv, ring_send, ring_recv, z_send, z_recv):
    gx, gy = lax.axis_index("gx"), lax.axis_index("gy")
    core, z = gx % 2, (gx // 2) % NZ_RING
    x, y = gy // 2, (gy % 2) * 2 + gx // (2 * NZ_RING)
    n_gx, n_gy = 2 * 2 * NZ_RING, 2 * NX_RING
    sibling = device_at(1 - core, x, y, z)

    def at_x(d):
        return device_at(core, (x + d) % NX_RING, y, z)

    def at_y(d):
        return device_at(core, x, (y + d) % NY_RING, z)

    def at_z(d):
        return device_at(core, x, y, (z + d) % NZ_RING)

    before_x, after_x = ((gx + n_gx - 1) % n_gx, gy), ((gx + 1) % n_gx, gy)
    before_y, after_y = (gx, (gy + n_gy - 1) % n_gy), (gx, (gy + 1) % n_gy)

    loads = [pltpu.make_async_copy(ev_in, ev, load.at[0]), pltpu.make_async_copy(links_in, links, load.at[1])]
    for copy in loads:
        copy.start()
    barrier = pltpu.get_barrier_semaphore()
    peers = [before_x, after_x, before_y, after_y, sibling]
    peers += [at_x(d) for d in range(1, NX_RING)]
    peers += [at_y(d) for d in range(1, NY_RING)]
    peers += [at_z(d) for d in range(1, NZ_RING)]
    for peer in peers:
        pl.semaphore_signal(barrier, inc=1, device_id=peer, device_id_type=MESH)

    nz, nx, ny, vecs = ev.shape[2:]
    planes = nz * nx
    inner, edge_x = 6 * nz * (nx - 1) * ny, 6 * nz * ny
    main = inner + edge_x
    faces = 6 * planes
    loads[0].wait()

    def take_faces(zz, carry):
        for p in range(2):
            for c in range(3):
                for xx in range(nx):
                    value = ev[p, c, zz, xx].astype(F32)
                    row = pl.ds((p * 3 + c) * planes + zz * nx + xx, 1)
                    face_f[0, row, :] = value[0:1, :]
                    face_f[1, row, :] = value[ny - 1 : ny, :]
        return carry

    lax.fori_loop(0, nz, take_faces, 0)
    face[...] = face_f[0].astype(BF16)

    vt[:, :inner] = ev[:, :, :, : nx - 1].reshape(inner, vecs).T
    vt[:, inner:main] = ev[:, :, :, nx - 1].reshape(edge_x, vecs).T
    pad = jnp.zeros((vt.shape[1] - main - faces, vecs), F32)
    vt[:, main:] = jnp.concatenate([face_f[1], pad], axis=0).T.astype(BF16)
    for q in range(2):
        right[0, q, main + faces :, :] = pad.astype(BF16)
    pl.semaphore_wait(barrier, len(peers))

    started = []

    def send(src, dst, s_sem, r_sem, to):
        copy = pltpu.make_async_remote_copy(
            src_ref=src, dst_ref=dst, send_sem=s_sem, recv_sem=r_sem, device_id=to, device_id_type=MESH
        )
        copy.start()
        started.append(copy)
        return copy

    copy_y = send(face, halo_y, halo_send.at[0], halo_recv.at[0], before_y)
    copies_x = [
        send(ev_in.at[:, :, zz, 0], halo_x.at[:, :, zz], halo_send.at[1 + zz], halo_recv.at[1 + zz], before_x)
        for zz in range(nz)
    ]

    def colour(h, columns, source, row_of):
        coef = [jnp.broadcast_to(column, (column.shape[0], LANES)) for column in columns]
        for lane in range(vecs // LANES):
            at = slice(lane * LANES, (lane + 1) * LANES)
            v = [[source(p, c, at) for c in range(3)] for p in range(2)]
            for a in range(3):
                re = im = None
                for b in range(3):
                    u_re, u_im = coef[a * 3 + b], coef[9 + a * 3 + b]
                    t_re = u_re * v[0][b] - u_im * v[1][b]
                    t_im = u_re * v[1][b] + u_im * v[0][b]
                    re = t_re if re is None else re + t_re
                    im = t_im if im is None else im + t_im
                re, im = re.astype(BF16), im.astype(BF16)
                right[h, 0, row_of(0, a), at] = re
                right[h, 0, row_of(1, a), at] = im
                right[h, 1, row_of(0, a), at] = im
                right[h, 1, row_of(1, a), at] = -re

    def plane_columns(h, zz, xx):
        columns = links[pl.ds((1 - h) * 18 * planes + zz * nx + xx, 18, stride=planes), :].T
        return [columns[:, i : i + 1] for i in range(18)]

    def plane_rows(zz, xx):
        def row_of(p, c):
            if xx < nx - 1:
                start = (((p * 3 + c) * nz + zz) * (nx - 1) + xx) * ny
            else:
                start = inner + ((p * 3 + c) * nz + zz) * ny
            return pl.ds(pl.multiple_of(start, ny), ny)

        return row_of

    def hop_x_inner(zz, carry):
        for xx in range(nx - 1):
            colour(1, plane_columns(1, zz, xx), lambda p, c, at: ev[p, c, zz, xx + 1, :, at].astype(F32),
                   plane_rows(zz, xx))
        return carry

    def hop_x_last():
        for zz in range(nz):
            colour(1, plane_columns(1, zz, nx - 1), lambda p, c, at: halo_x[p, c, zz, :, at].astype(F32),
                   plane_rows(zz, nx - 1))

    def hop_y_main(zz, carry):
        last = lax.broadcasted_iota(jnp.int32, (ny, LANES), 0) == ny - 1
        for xx in range(nx):
            def source(p, c, at):
                return jnp.where(last, 0.0, pltpu.roll(ev[p, c, zz, xx, :, at].astype(F32), ny - 1, 0))

            colour(0, plane_columns(0, zz, xx), source, plane_rows(zz, xx))
        return carry

    def hop_y_edge():
        first_row = 18 * planes
        columns = [links[first_row + i * planes : first_row + (i + 1) * planes, ny - 1 : ny] for i in range(18)]

        def row_of(p, c):
            start = main + (p * 3 + c) * planes
            return slice(start, start + planes)

        def source(p, c, at):
            return halo_y[(p * 3 + c) * planes : (p * 3 + c + 1) * planes, at].astype(F32)

        colour(0, columns, source, row_of)

    def gram(h, q, low, high):
        lhs = vt[:, low:high]
        for j in range(vecs // (2 * LANES)):
            rhs = right[h, q, low:high, j * 2 * LANES : (j + 1) * 2 * LANES]
            value = jnp.dot(lhs, rhs, preferred_element_type=F32) * norm
            for half in range(2):
                yield slice((2 * j + half) * vecs, (2 * j + half + 1) * vecs), value[:, half * LANES : (half + 1) * LANES]

    def gram_x_inner():
        for at, value in gram(1, 1 - core, 0, inner):
            other[at, :] = value
        for at, value in gram(1, core, 0, inner):
            own[1, at, :] = value

    def to_core(h):
        return send(send0.at[h], recv0.at[h], core_send.at[h, 0], core_recv.at[h, 0], sibling)

    def gram_x_other():
        for at, value in gram(1, 1 - core, inner, main):
            send0[1, at, :] = (other[at, :] + value).astype(BF16)
        return to_core(1)

    def gram_x_own():
        for at, value in gram(1, core, inner, main):
            own[1, at, :] += value

    def gram_y_other():
        for at, value in gram(0, 1 - core, 0, vt.shape[1]):
            send0[0, at, :] = value.astype(BF16)
        return to_core(0)

    def gram_y_own():
        for at, value in gram(0, core, 0, vt.shape[1]):
            own[0, at, :] = value

    first = ((x, at_x), (y, at_y))
    second = ((y, at_y), (x, at_x))
    half = own.shape[1]
    part, len1, len2, len3 = half // 2, half // 8, half // 32, half // 256

    def start1(h, copy):
        copy.wait_recv()
        total = own[h] + recv0[h].astype(F32)
        own[h] = total
        send1[h] = total.astype(BF16)
        return [
            [
                send(send1.at[h, pl.ds(s * part + (first[s][0] + d) % 4 * len1, len1)], recv1.at[h, s, d - 1],
                     ring_send.at[h, 0, s, d - 1], ring_recv.at[h, 0, s, d - 1], first[s][1](d))
                for d in range(1, 4)
            ]
            for s in range(2)
        ]

    def start2(h, copies):
        result = []
        for s in range(2):
            total = own[h, pl.ds(s * part + first[s][0] * len1, len1)]
            for d, copy in enumerate(copies[s]):
                copy.wait_recv()
                total = total + recv1[h, s, d].astype(F32)
            own2[h, s] = total
            send2[h, s] = total.astype(BF16)
            place, at = second[s]
            result.append([
                send(send2.at[h, s, pl.ds((place + d) % 4 * len2, len2)], recv2.at[h, s, d - 1],
                     ring_send.at[h, 1, s, d - 1], ring_recv.at[h, 1, s, d - 1], at(d))
                for d in range(1, 4)
            ])
        return result

    def start3(h, copies):
        totals = []
        for s in range(2):
            total = own2[h, s, pl.ds(second[s][0] * len2, len2)]
            for d, copy in enumerate(copies[s]):
                copy.wait_recv()
                total = total + recv2[h, s, d].astype(F32)
            totals.append(total)
        total = jnp.concatenate(
            [totals[s][i * len3 : (i + 1) * len3] for i in range(NZ_RING) for s in range(2)], axis=0
        )
        own3[h] = total
        send3[h] = total.astype(BF16)
        return [
            send(send3.at[h, pl.ds((z + d) % NZ_RING * 2 * len3, 2 * len3)], recv3.at[h, d - 1],
                 z_send.at[h, 0, d - 1], z_recv.at[h, 0, d - 1], at_z(d))
            for d in range(1, NZ_RING)
        ]

    def base(s):
        b0 = core * half + s * part
        b1 = b0 + first[s][0] * len1
        return b0, b1, b1 + second[s][0] * len2

    def gather3(h, copies):
        place = pl.ds(z * 2 * len3, 2 * len3)
        total = own3[h, place]
        for d, copy in enumerate(copies):
            copy.wait_recv()
            total = total + recv3[h, d].astype(F32)
        done3[h, place] = total.astype(BF16)
        return [
            send(done3.at[h, place], done3.at[h, place], z_send.at[h, 1, d - 1], z_recv.at[h, 1, d - 1], at_z(d))
            for d in range(1, NZ_RING)
        ]

    def gather2(h, copies):
        for copy in copies:
            copy.wait_recv()
        value = done3[h].astype(F32)
        result = []
        for s in range(2):
            place = pl.ds(base(s)[2], len2)
            out[h, place] = jnp.concatenate(
                [value[(2 * i + s) * len3 : (2 * i + s + 1) * len3] for i in range(NZ_RING)], axis=0
            ).astype(BF16)
            result += [
                send(out.at[h, place], out.at[h, place], ring_send.at[h, 2, s, d - 1], ring_recv.at[h, 2, s, d - 1],
                     second[s][1](d))
                for d in range(1, 4)
            ]
        return result

    def to_sibling(h, s, d, place):
        return send(out.at[h, place], out.at[h, place], core_send.at[h, 1 + 4 * s + d], core_recv.at[h, 1 + 4 * s + d],
                    sibling)

    def gather1(h, copies):
        for copy in copies:
            copy.wait_recv()
        rings, across = [], []
        for s in range(2):
            place = pl.ds(base(s)[1], len1)
            rings.append([
                send(out.at[h, place], out.at[h, place], ring_send.at[h, 3, s, d - 1], ring_recv.at[h, 3, s, d - 1],
                     first[s][1](d))
                for d in range(1, 4)
            ])
            across.append(to_sibling(h, s, 0, place))
        return rings, across

    def gather0(h, both):
        rings, across = both
        for d in (1, 3, 2):
            for s in range(2):
                rings[s][d - 1].wait_recv()
                place = pl.ds(base(s)[0] + (first[s][0] + 4 - d) % 4 * len1, len1)
                across.append(to_sibling(h, s, d, place))
        return across

    loads[1].wait()
    lax.fori_loop(0, nz, hop_x_inner, 0)
    gram_x_inner()
    lax.fori_loop(0, nz, hop_y_main, 0)
    for copy in copies_x:
        copy.wait_recv()
    hop_x_last()
    a = gram_x_other()
    gram_x_own()
    copy_y.wait_recv()
    hop_y_edge()
    b = gram_y_other()
    a = start1(1, a)
    gram_y_own()
    b = start1(0, b)
    for step in (start2, start3, gather3, gather2, gather1, gather0):
        a = step(1, a)
        b = step(0, b)
    for copy in a + b:
        copy.wait_recv()
    for copy in started:
        copy.wait_send()


def contract_kernel(directions, spins, g, peram, elementals, contracted, products):
    gx = lax.axis_index("gx")
    vecs = peram.shape[-1] // 4
    rows = peram.shape[1]
    own_rows = elementals.shape[2]
    pieces = [peram[p].astype(F32)[:, t * vecs : (t + 1) * vecs] for p in range(2) for t in range(4)]
    pick = lax.broadcasted_iota(jnp.int32, (own_rows, vecs), 1) == gx * own_rows + lax.broadcasted_iota(
        jnp.int32, (own_rows, vecs), 0
    )
    lhs = jnp.concatenate(pieces + [jnp.where(pick, 1.0, 0.0)], axis=0).astype(BF16)
    m = 4 * rows
    for h in range(2):
        parts = []
        for q in range(2):
            blocks = [g[h, (q * 4 + j) * vecs : (q * 4 + j + 1) * vecs, :] for j in range(4)]
            parts.append(jnp.concatenate(blocks, axis=1))
        re = jnp.dot(lhs, parts[0], preferred_element_type=F32)
        im = jnp.dot(lhs, parts[1], preferred_element_type=F32)
        products[h, 0] = jnp.concatenate([re[:m] - im[m : 2 * m], re[2 * m :]], 0)
        products[h, 1] = jnp.concatenate([im[:m] + re[m : 2 * m], im[2 * m :]], 0)
        over = (((1,), (1,)), ((), ()))
        re = lax.dot_general(lhs, parts[0], over, preferred_element_type=F32)
        im = lax.dot_general(lhs, parts[1], over, preferred_element_type=F32)
        products[2 + h, 0] = jnp.concatenate([re[:m] + im[m : 2 * m], re[2 * m :]], 0)
        products[2 + h, 1] = jnp.concatenate([re[m : 2 * m] - im[:m], -im[2 * m :]], 0)
    for k in range(4):
        which = jnp.where(directions[k] % 2 == 0, directions[k] + 1, directions[k] - 1)
        for q in range(2):
            elementals[k, q] = products[which, q, m : m + own_rows, :]
            for u in range(4):
                row = pl.multiple_of(spins[u] * rows, rows)
                contracted[k, q, :, u * vecs : (u + 1) * vecs] = products[which, q, pl.ds(row, rows), :].astype(BF16)


def local(eigen_vecs, gauge_links, directions, spin_map, perambulator):
    reim, colours, nz, nx, ny, vecs = eigen_vecs.shape
    sites = nz * nx * ny * lax.axis_size("gx") * lax.axis_size("gy")
    norm = 1.0 / math.sqrt(3.0 * sites)
    ev = eigen_vecs
    links = gauge_links.reshape(-1, ny)
    half = vecs * vecs // LANES
    vmem = pl.BlockSpec(memory_space=pltpu.VMEM)
    faces = reim * colours * nz * nx
    summed = faces * ny + -(-faces // LANES) * LANES
    g = pl.pallas_call(
        lambda *refs: reduce_kernel(norm, *refs),
        out_shape=jax.ShapeDtypeStruct((2, 2 * half, LANES), BF16),
        in_specs=[pl.BlockSpec(memory_space=pltpu.HBM)] * 2,
        out_specs=vmem,
        scratch_shapes=[
            pltpu.VMEM(ev.shape, BF16),
            pltpu.VMEM(links.shape, F32),
            pltpu.VMEM((vecs, summed), BF16),
            pltpu.VMEM((2, 2, summed, vecs), BF16),
            pltpu.VMEM((2, faces, vecs), F32),
            pltpu.VMEM((faces, vecs), BF16),
            pltpu.VMEM((faces, vecs), BF16),
            pltpu.VMEM((reim, colours, nz, ny, vecs), BF16),
            pltpu.VMEM((2, half, LANES), BF16),
            pltpu.VMEM((2, half, LANES), F32),
            pltpu.VMEM((half, LANES), F32),
            pltpu.VMEM((2, half, LANES), BF16),
            pltpu.VMEM((2, half, LANES), BF16),
            pltpu.VMEM((2, 2, 3, half // 8, LANES), BF16),
            pltpu.VMEM((2, 2, half // 8, LANES), F32),
            pltpu.VMEM((2, 2, half // 8, LANES), BF16),
            pltpu.VMEM((2, 2, 3, half // 32, LANES), BF16),
            pltpu.VMEM((2, half // 16, LANES), F32),
            pltpu.VMEM((2, half // 16, LANES), BF16),
            pltpu.VMEM((2, NZ_RING - 1, half // 128, LANES), BF16),
            pltpu.VMEM((2, half // 16, LANES), BF16),
            pltpu.SemaphoreType.DMA((2,)),
            pltpu.SemaphoreType.DMA((1 + nz,)),
            pltpu.SemaphoreType.DMA((1 + nz,)),
            pltpu.SemaphoreType.DMA((2, 9)),
            pltpu.SemaphoreType.DMA((2, 9)),
            pltpu.SemaphoreType.DMA((2, 4, 2, 3)),
            pltpu.SemaphoreType.DMA((2, 4, 2, 3)),
            pltpu.SemaphoreType.DMA((2, 2, NZ_RING - 1)),
            pltpu.SemaphoreType.DMA((2, 2, NZ_RING - 1)),
        ],
        compiler_params=pltpu.CompilerParams(
            collective_id=0, has_side_effects=True, vmem_limit_bytes=48 * 2**20
        ),
        name="reduce",
    )(ev, links)
    rows = perambulator.shape[1]
    own_rows = vecs // lax.axis_size("gx")
    smem = pl.BlockSpec(memory_space=pltpu.SMEM)
    return pl.pallas_call(
        contract_kernel,
        out_shape=(
            jax.ShapeDtypeStruct((4, 2, own_rows, vecs), F32),
            jax.ShapeDtypeStruct((4, 2, rows, 4 * vecs), BF16),
        ),
        in_specs=[smem, smem, vmem, vmem],
        out_specs=(vmem, vmem),
        scratch_shapes=[pltpu.VMEM((4, 2, 4 * rows + own_rows, vecs), F32)],
        compiler_params=pltpu.CompilerParams(vmem_limit_bytes=32 * 2**20),
        name="contract",
    )(directions, spin_map, g, perambulator)


def solution(mesh):
    in_specs = (
        P(None, None, None, "gx", "gy", None),
        P(None, None, None, None, None, "gx", "gy"),
        P(),
        P(),
        P(None, ("gx", "gy"), None),
    )
    out_specs = (P(None, None, "gx", None), P(None, None, ("gx", "gy"), None))
    return jax.shard_map(local, mesh=mesh, in_specs=in_specs, out_specs=out_specs, check_vma=False)
```

```python
import math

import jax
import jax.numpy as jnp
from jax import lax
from jax.experimental import pallas as pl
from jax.experimental.pallas import tpu as pltpu
from jax.sharding import PartitionSpec as P

MESH = pl.DeviceIdType.MESH
F32 = jnp.float32
BF16 = jnp.bfloat16
NX_RING, NY_RING, NZ_RING, CORES = 4, 4, 8, 2
LANES = 128


def device_at(core, x, y, z):
    return (((y % 2) * NZ_RING + z) * CORES + core, x * 2 + y // 2)


def reduce_kernel(norm, ev_in, links_in, peram_in, parts, picks, products, out, ev, links, peram, lhs_f, lhs, vt, right, face_f, face, halo_y, halo_x, send0, own, other, recv0,
                  send1, recv1, own2, send2, recv2, own3, send3, recv3, done3, there,
                  load, peram_send, peram_recv, halo_send, halo_recv, core_send, core_recv, ring_send, ring_recv, z_send, z_recv):
    gx, gy = lax.axis_index("gx"), lax.axis_index("gy")
    core, z = gx % 2, (gx // 2) % NZ_RING
    x, y = gy // 2, (gy % 2) * 2 + gx // (2 * NZ_RING)
    n_gx, n_gy = 2 * 2 * NZ_RING, 2 * NX_RING
    sibling = device_at(1 - core, x, y, z)

    def at_x(d):
        return device_at(core, (x + d) % NX_RING, y, z)

    def at_y(d):
        return device_at(core, x, (y + d) % NY_RING, z)

    def at_z(d):
        return device_at(core, x, y, (z + d) % NZ_RING)

    before_x, after_x = ((gx + n_gx - 1) % n_gx, gy), ((gx + 1) % n_gx, gy)
    before_y, after_y = (gx, (gy + n_gy - 1) % n_gy), (gx, (gy + 1) % n_gy)

    loads = [
        pltpu.make_async_copy(ev_in, ev, load.at[0]),
        pltpu.make_async_copy(links_in, links, load.at[1]),
        pltpu.make_async_copy(peram_in, peram.at[0], load.at[2]),
    ]
    for copy in loads:
        copy.start()
    barrier = pltpu.get_barrier_semaphore()
    peers = [before_x, after_x, before_y, after_y, sibling]
    peers += [at_x(d) for d in range(1, NX_RING)]
    peers += [at_y(d) for d in range(1, NY_RING)]
    peers += [at_z(d) for d in range(1, NZ_RING)]
    for peer in peers:
        pl.semaphore_signal(barrier, inc=1, device_id=peer, device_id_type=MESH)

    nz, nx, ny, vecs = ev.shape[2:]
    planes = nz * nx
    inner, edge_x = 6 * nz * (nx - 1) * ny, 6 * nz * ny
    main = inner + edge_x
    faces = 6 * planes
    loads[0].wait()

    def take_faces(zz, carry):
        for p in range(2):
            for c in range(3):
                for xx in range(nx):
                    value = ev[p, c, zz, xx].astype(F32)
                    row = pl.ds((p * 3 + c) * planes + zz * nx + xx, 1)
                    face_f[0, row, :] = value[0:1, :]
                    face_f[1, row, :] = value[ny - 1 : ny, :]
        return carry

    lax.fori_loop(0, nz, take_faces, 0)
    face[...] = face_f[0].astype(BF16)

    vt[:, :inner] = ev[:, :, :, : nx - 1].reshape(inner, vecs).T
    vt[:, inner:main] = ev[:, :, :, nx - 1].reshape(edge_x, vecs).T
    pad = jnp.zeros((vt.shape[1] - main - faces, vecs), F32)
    vt[:, main:] = jnp.concatenate([face_f[1], pad], axis=0).T.astype(BF16)
    for q in range(2):
        right[0, q, main + faces :, :] = pad.astype(BF16)
    pl.semaphore_wait(barrier, len(peers))

    started = []

    def send(src, dst, s_sem, r_sem, to):
        copy = pltpu.make_async_remote_copy(
            src_ref=src, dst_ref=dst, send_sem=s_sem, recv_sem=r_sem, device_id=to, device_id_type=MESH
        )
        copy.start()
        started.append(copy)
        return copy

    copy_y = send(face, halo_y, halo_send.at[0], halo_recv.at[0], before_y)
    copies_x = [
        send(ev_in.at[:, :, zz, 0], halo_x.at[:, :, zz], halo_send.at[1 + zz], halo_recv.at[1 + zz], before_x)
        for zz in range(nz)
    ]

    copy_p = send(peram_in, peram.at[1], peram_send, peram_recv, sibling)

    def colour(h, columns, source, row_of):
        coef = [jnp.broadcast_to(column, (column.shape[0], LANES)) for column in columns]
        for lane in range(vecs // LANES):
            at = slice(lane * LANES, (lane + 1) * LANES)
            v = [[source(p, c, at) for c in range(3)] for p in range(2)]
            for a in range(3):
                re = im = None
                for b in range(3):
                    u_re, u_im = coef[a * 3 + b], coef[9 + a * 3 + b]
                    t_re = u_re * v[0][b] - u_im * v[1][b]
                    t_im = u_re * v[1][b] + u_im * v[0][b]
                    re = t_re if re is None else re + t_re
                    im = t_im if im is None else im + t_im
                re, im = re.astype(BF16), im.astype(BF16)
                right[h, 0, row_of(0, a), at] = re
                right[h, 0, row_of(1, a), at] = im
                right[h, 1, row_of(0, a), at] = im
                right[h, 1, row_of(1, a), at] = -re

    def plane_columns(h, zz, xx):
        columns = links[pl.ds((1 - h) * 18 * planes + zz * nx + xx, 18, stride=planes), :].T
        return [columns[:, i : i + 1] for i in range(18)]

    def plane_rows(zz, xx):
        def row_of(p, c):
            if xx < nx - 1:
                start = (((p * 3 + c) * nz + zz) * (nx - 1) + xx) * ny
            else:
                start = inner + ((p * 3 + c) * nz + zz) * ny
            return slice(start, start + ny) if isinstance(start, int) else pl.ds(pl.multiple_of(start, ny), ny)

        return row_of

    def hop_x_inner(zz, carry):
        for xx in range(nx - 1):
            colour(1, plane_columns(1, zz, xx), lambda p, c, at: ev[p, c, zz, xx + 1, :, at].astype(F32),
                   plane_rows(zz, xx))
        return carry

    def hop_x_last():
        for zz in range(nz):
            colour(1, plane_columns(1, zz, nx - 1), lambda p, c, at: halo_x[p, c, zz, :, at].astype(F32),
                   plane_rows(zz, nx - 1))

    def hop_y_main(zz, carry):
        last = lax.broadcasted_iota(jnp.int32, (ny, LANES), 0) == ny - 1
        for xx in range(nx):
            def source(p, c, at):
                return jnp.where(last, 0.0, pltpu.roll(ev[p, c, zz, xx, :, at].astype(F32), ny - 1, 0))

            colour(0, plane_columns(0, zz, xx), source, plane_rows(zz, xx))
        return carry

    def hop_y_edge():
        first_row = 18 * planes
        columns = [links[first_row + i * planes : first_row + (i + 1) * planes, ny - 1 : ny] for i in range(18)]

        def row_of(p, c):
            start = main + (p * 3 + c) * planes
            return slice(start, start + planes)

        def source(p, c, at):
            return halo_y[(p * 3 + c) * planes : (p * 3 + c + 1) * planes, at].astype(F32)

        colour(0, columns, source, row_of)

    def gram(h, q, low, high):
        lhs = vt[:, low:high]
        for j in range(vecs // (2 * LANES)):
            rhs = right[h, q, low:high, j * 2 * LANES : (j + 1) * 2 * LANES]
            value = jnp.dot(lhs, rhs, preferred_element_type=F32) * norm
            for half in range(2):
                yield slice((2 * j + half) * vecs, (2 * j + half + 1) * vecs), value[:, half * LANES : (half + 1) * LANES]

    def gram_x_inner():
        for at, value in gram(1, 1 - core, 0, inner):
            other[at, :] = value
        for at, value in gram(1, core, 0, inner):
            own[1, at, :] = value

    def to_core(h):
        return send(send0.at[h], recv0.at[h], core_send.at[h, 0], core_recv.at[h, 0], sibling)

    def gram_x_other():
        for at, value in gram(1, 1 - core, inner, main):
            send0[1, at, :] = (other[at, :] + value).astype(BF16)
        return to_core(1)

    def gram_x_own():
        for at, value in gram(1, core, inner, main):
            own[1, at, :] += value

    def gram_y_other():
        for at, value in gram(0, 1 - core, 0, vt.shape[1]):
            send0[0, at, :] = value.astype(BF16)
        return to_core(0)

    def gram_y_own():
        for at, value in gram(0, core, 0, vt.shape[1]):
            own[0, at, :] = value

    first = ((x, at_x), (y, at_y))
    second = ((y, at_y), (x, at_x))
    half = own.shape[1]
    part, len1, len2, len3 = half // 2, half // 8, half // 32, half // 256

    def start1(h, copy):
        copy.wait_recv()
        total = own[h] + recv0[h].astype(F32)
        own[h] = total
        send1[h] = total.astype(BF16)
        return [
            [
                send(send1.at[h, pl.ds(s * part + (first[s][0] + d) % 4 * len1, len1)], recv1.at[h, s, d - 1],
                     ring_send.at[h, 0, s, d - 1], ring_recv.at[h, 0, s, d - 1], first[s][1](d))
                for d in range(1, 4)
            ]
            for s in range(2)
        ]

    def start2(h, copies):
        result = []
        for s in range(2):
            total = own[h, pl.ds(s * part + first[s][0] * len1, len1)]
            for d, copy in enumerate(copies[s]):
                copy.wait_recv()
                total = total + recv1[h, s, d].astype(F32)
            own2[h, s] = total
            send2[h, s] = total.astype(BF16)
            place, at = second[s]
            result.append([
                send(send2.at[h, s, pl.ds((place + d) % 4 * len2, len2)], recv2.at[h, s, d - 1],
                     ring_send.at[h, 1, s, d - 1], ring_recv.at[h, 1, s, d - 1], at(d))
                for d in range(1, 4)
            ])
        return result

    def start3(h, copies):
        totals = []
        for s in range(2):
            total = own2[h, s, pl.ds(second[s][0] * len2, len2)]
            for d, copy in enumerate(copies[s]):
                copy.wait_recv()
                total = total + recv2[h, s, d].astype(F32)
            totals.append(total)
        total = jnp.concatenate(
            [totals[s][i * len3 : (i + 1) * len3] for i in range(NZ_RING) for s in range(2)], axis=0
        )
        own3[h] = total
        send3[h] = total.astype(BF16)
        return [
            send(send3.at[h, pl.ds((z + d) % NZ_RING * 2 * len3, 2 * len3)], recv3.at[h, d - 1],
                 z_send.at[h, 0, d - 1], z_recv.at[h, 0, d - 1], at_z(d))
            for d in range(1, NZ_RING)
        ]

    def base(s):
        b0 = s * part
        b1 = b0 + first[s][0] * len1
        return b0, b1, b1 + second[s][0] * len2

    def gather3(h, copies):
        place = pl.ds(z * 2 * len3, 2 * len3)
        total = own3[h, place]
        for d, copy in enumerate(copies):
            copy.wait_recv()
            total = total + recv3[h, d].astype(F32)
        done3[h, place] = total.astype(BF16)
        return [
            send(done3.at[h, place], done3.at[h, place], z_send.at[h, 1, d - 1], z_recv.at[h, 1, d - 1], at_z(d))
            for d in range(1, NZ_RING)
        ]

    def gather2(h, copies):
        for copy in copies:
            copy.wait_recv()
        value = done3[h].astype(F32)
        result = []
        for s in range(2):
            place = pl.ds(base(s)[2], len2)
            out[h, place] = jnp.concatenate(
                [value[(2 * i + s) * len3 : (2 * i + s + 1) * len3] for i in range(NZ_RING)], axis=0
            ).astype(BF16)
            result += [
                send(out.at[h, place], out.at[h, place], ring_send.at[h, 2, s, d - 1], ring_recv.at[h, 2, s, d - 1],
                     second[s][1](d))
                for d in range(1, 4)
            ]
        return result

    def gather1(h, copies):
        for copy in copies:
            copy.wait_recv()
        result = []
        for s in range(2):
            place = pl.ds(base(s)[1], len1)
            result += [
                send(out.at[h, place], out.at[h, place], ring_send.at[h, 3, s, d - 1], ring_recv.at[h, 3, s, d - 1],
                     first[s][1](d))
                for d in range(1, 4)
            ]
        return result

    m = lhs.shape[1] - vecs // n_gx
    own_rows = lhs.shape[1] - m

    def make_lhs():
        rows = peram.shape[2]
        for who in range(2):
            place = gx if who == 0 else gx + 1 - 2 * core
            for p in range(2):
                value = peram[who, p].astype(F32)
                for t in range(4):
                    start = (p * 4 + t) * rows
                    lhs_f[who, start : start + rows, :] = value[:, t * vecs : (t + 1) * vecs]
            column = lax.broadcasted_iota(jnp.int32, (own_rows, vecs), 1)
            row = lax.broadcasted_iota(jnp.int32, (own_rows, vecs), 0)
            lhs_f[who, m:, :] = jnp.where(column == place * own_rows + row, 1.0, 0.0)
        lhs[...] = lhs_f[...].astype(BF16)

    def contract(h, copies):
        for copy in copies:
            copy.wait_recv()
        blocks = out.shape[1] // vecs
        value = jnp.concatenate([out[h, j * vecs : (j + 1) * vecs, :] for j in range(blocks)], axis=1)
        across = (((1,), (1,)), ((), ()))
        there[h, 0] = jnp.dot(lhs[1], value, preferred_element_type=F32)
        there[h, 1] = lax.dot_general(lhs[1], value, across, preferred_element_type=F32)
        copy = send(there.at[h], products.at[core, h], core_send.at[h, 1], core_recv.at[h, 1], sibling)
        products[core, h, 0] = jnp.dot(lhs[0], value, preferred_element_type=F32)
        products[core, h, 1] = lax.dot_general(lhs[0], value, across, preferred_element_type=F32)
        return [copy]

    def combine(h, copies):
        copies[0].wait_recv()
        low = m // 2
        re, im = products[0, h, 0], products[1, h, 0]
        parts[h, 0] = (re[:low] - im[low:m]).astype(BF16)
        parts[h, 1] = (im[:low] + re[low:m]).astype(BF16)
        picks[h, 0] = re[m:]
        picks[h, 1] = im[m:]
        re, im = products[0, h, 1], products[1, h, 1]
        parts[2 + h, 0] = (re[:low] + im[low:m]).astype(BF16)
        parts[2 + h, 1] = (re[low:m] - im[:low]).astype(BF16)
        picks[2 + h, 0] = re[m:]
        picks[2 + h, 1] = -im[m:]

    loads[1].wait()
    for zz in range(nz):
        hop_x_inner(zz, 0)
    gram_x_inner()
    for zz in range(nz):
        hop_y_main(zz, 0)
    copy_y.wait_recv()
    hop_y_edge()
    b = gram_y_other()
    for copy in copies_x:
        copy.wait_recv()
    hop_x_last()
    a = gram_x_other()
    gram_y_own()
    b = start1(0, b)
    gram_x_own()
    a = start1(1, a)
    loads[2].wait()
    copy_p.wait_recv()
    make_lhs()
    for step in (start2, start3, gather3, gather2, gather1, contract):
        b = step(0, b)
        a = step(1, a)
    combine(0, b)
    combine(1, a)
    for copy in started:
        copy.wait_send()


def place_kernel(directions, spins, parts, picks, elementals, contracted):
    rows, vecs = contracted.shape[2], elementals.shape[3]
    for k in range(4):
        which = jnp.where(directions[k] % 2 == 0, directions[k] + 1, directions[k] - 1)
        elementals[k] = picks[which]
        for q in range(2):
            for u in range(4):
                contracted[k, q, :, u * vecs : (u + 1) * vecs] = parts[which, q, spins[u]]


def local(eigen_vecs, gauge_links, directions, spin_map, perambulator):
    reim, colours, nz, nx, ny, vecs = eigen_vecs.shape
    sites = nz * nx * ny * lax.axis_size("gx") * lax.axis_size("gy")
    norm = 1.0 / math.sqrt(3.0 * sites)
    ev = eigen_vecs
    links = gauge_links.reshape(-1, ny)
    half = vecs * vecs // LANES
    vmem = pl.BlockSpec(memory_space=pltpu.VMEM)
    faces = reim * colours * nz * nx
    summed = faces * ny + -(-faces // LANES) * LANES
    rows = perambulator.shape[1]
    own_rows = vecs // lax.axis_size("gx")
    lhs_rows = 8 * rows + own_rows
    parts, picks = pl.pallas_call(
        lambda *refs: reduce_kernel(norm, *refs),
        out_shape=(
            jax.ShapeDtypeStruct((4, 2, 4 * rows, vecs), BF16),
            jax.ShapeDtypeStruct((4, 2, own_rows, vecs), F32),
        ),
        in_specs=[pl.BlockSpec(memory_space=pltpu.HBM)] * 3,
        out_specs=(vmem, vmem),
        scratch_shapes=[
            pltpu.VMEM((2, 2, 2, lhs_rows, vecs), F32),
            pltpu.VMEM((2, half, LANES), BF16),
            pltpu.VMEM(ev.shape, BF16),
            pltpu.VMEM(links.shape, F32),
            pltpu.VMEM((2, *perambulator.shape), BF16),
            pltpu.VMEM((2, lhs_rows, vecs), F32),
            pltpu.VMEM((2, lhs_rows, vecs), BF16),
            pltpu.VMEM((vecs, summed), BF16),
            pltpu.VMEM((2, 2, summed, vecs), BF16),
            pltpu.VMEM((2, faces, vecs), F32),
            pltpu.VMEM((faces, vecs), BF16),
            pltpu.VMEM((faces, vecs), BF16),
            pltpu.VMEM((reim, colours, nz, ny, vecs), BF16),
            pltpu.VMEM((2, half, LANES), BF16),
            pltpu.VMEM((2, half, LANES), F32),
            pltpu.VMEM((half, LANES), F32),
            pltpu.VMEM((2, half, LANES), BF16),
            pltpu.VMEM((2, half, LANES), BF16),
            pltpu.VMEM((2, 2, 3, half // 8, LANES), BF16),
            pltpu.VMEM((2, 2, half // 8, LANES), F32),
            pltpu.VMEM((2, 2, half // 8, LANES), BF16),
            pltpu.VMEM((2, 2, 3, half // 32, LANES), BF16),
            pltpu.VMEM((2, half // 16, LANES), F32),
            pltpu.VMEM((2, half // 16, LANES), BF16),
            pltpu.VMEM((2, NZ_RING - 1, half // 128, LANES), BF16),
            pltpu.VMEM((2, half // 16, LANES), BF16),
            pltpu.VMEM((2, 2, lhs_rows, vecs), F32),
            pltpu.SemaphoreType.DMA((3,)),
            pltpu.SemaphoreType.DMA,
            pltpu.SemaphoreType.DMA,
            pltpu.SemaphoreType.DMA((1 + nz,)),
            pltpu.SemaphoreType.DMA((1 + nz,)),
            pltpu.SemaphoreType.DMA((2, 2)),
            pltpu.SemaphoreType.DMA((2, 2)),
            pltpu.SemaphoreType.DMA((2, 4, 2, 3)),
            pltpu.SemaphoreType.DMA((2, 4, 2, 3)),
            pltpu.SemaphoreType.DMA((2, 2, NZ_RING - 1)),
            pltpu.SemaphoreType.DMA((2, 2, NZ_RING - 1)),
        ],
        compiler_params=pltpu.CompilerParams(
            collective_id=0, has_side_effects=True, vmem_limit_bytes=int(53.35 * 2**20)
        ),
        name="reduce",
    )(ev, links, perambulator)
    smem = pl.BlockSpec(memory_space=pltpu.SMEM)
    return pl.pallas_call(
        place_kernel,
        out_shape=(
            jax.ShapeDtypeStruct((4, 2, own_rows, vecs), F32),
            jax.ShapeDtypeStruct((4, 2, rows, 4 * vecs), BF16),
        ),
        in_specs=[smem, smem, vmem, vmem],
        out_specs=(vmem, vmem),
        compiler_params=pltpu.CompilerParams(vmem_limit_bytes=32 * 2**20),
        name="place",
    )(directions, spin_map, parts.reshape(4, 2, 4, rows, vecs), picks)


def solution(mesh):
    in_specs = (
        P(None, None, None, "gx", "gy", None),
        P(None, None, None, None, None, "gx", "gy"),
        P(),
        P(),
        P(None, ("gx", "gy"), None),
    )
    out_specs = (P(None, None, "gx", None), P(None, None, ("gx", "gy"), None))
    return jax.shard_map(local, mesh=mesh, in_specs=in_specs, out_specs=out_specs, check_vma=False)
```

```python
import math

import jax
import jax.numpy as jnp
from jax import lax
from jax.experimental import pallas as pl
from jax.experimental.pallas import tpu as pltpu
from jax.sharding import PartitionSpec as P

MESH = pl.DeviceIdType.MESH
F32 = jnp.float32
BF16 = jnp.bfloat16
NX_RING, NY_RING, NZ_RING, CORES = 4, 4, 8, 2
LANES = 128


def device_at(core, x, y, z):
    return (((y % 2) * NZ_RING + z) * CORES + core, x * 2 + y // 2)


def reduce_kernel(norm, ev_in, links_in, peram_in, parts, picks, products, out, ev, links, peram, lhs_f, lhs, vt, right, face_f, face, halo_y, halo_x, send0, own, other, recv0,
                  send1, recv1, own2, send2, recv2, own3, send3, recv3, done3, there,
                  load, peram_send, peram_recv, halo_send, halo_recv, core_send, core_recv, ring_send, ring_recv, z_send, z_recv):
    gx, gy = lax.axis_index("gx"), lax.axis_index("gy")
    core, z = gx % 2, (gx // 2) % NZ_RING
    x, y = gy // 2, (gy % 2) * 2 + gx // (2 * NZ_RING)
    n_gx, n_gy = 2 * 2 * NZ_RING, 2 * NX_RING
    sibling = device_at(1 - core, x, y, z)

    def at_x(d):
        return device_at(core, (x + d) % NX_RING, y, z)

    def at_y(d):
        return device_at(core, x, (y + d) % NY_RING, z)

    def at_z(d):
        return device_at(core, x, y, (z + d) % NZ_RING)

    before_x, after_x = ((gx + n_gx - 1) % n_gx, gy), ((gx + 1) % n_gx, gy)
    before_y, after_y = (gx, (gy + n_gy - 1) % n_gy), (gx, (gy + 1) % n_gy)

    loads = [
        pltpu.make_async_copy(ev_in, ev, load.at[0]),
        pltpu.make_async_copy(links_in, links, load.at[1]),
        pltpu.make_async_copy(peram_in, peram.at[0], load.at[2]),
    ]
    for copy in loads:
        copy.start()
    barrier = pltpu.get_barrier_semaphore()
    peers = [before_x, after_x, before_y, after_y, sibling]
    peers += [at_x(d) for d in range(1, NX_RING)]
    peers += [at_y(d) for d in range(1, NY_RING)]
    peers += [at_z(d) for d in range(1, NZ_RING)]
    for peer in peers:
        pl.semaphore_signal(barrier, inc=1, device_id=peer, device_id_type=MESH)

    nz, nx, ny, vecs = ev.shape[2:]
    planes = nz * nx
    inner, edge_x = 6 * nz * (nx - 1) * ny, 6 * nz * ny
    main = inner + edge_x
    faces = 6 * planes
    loads[0].wait()

    def take_faces(zz, carry):
        for p in range(2):
            for c in range(3):
                for xx in range(nx):
                    value = ev[p, c, zz, xx].astype(F32)
                    row = pl.ds((p * 3 + c) * planes + zz * nx + xx, 1)
                    face_f[0, row, :] = value[0:1, :]
                    face_f[1, row, :] = value[ny - 1 : ny, :]
        return carry

    lax.fori_loop(0, nz, take_faces, 0)
    face[...] = face_f[0].astype(BF16)

    vt[:, :inner] = ev[:, :, :, : nx - 1].reshape(inner, vecs).T
    vt[:, inner:main] = ev[:, :, :, nx - 1].reshape(edge_x, vecs).T
    pad = jnp.zeros((vt.shape[1] - main - faces, vecs), F32)
    vt[:, main:] = jnp.concatenate([face_f[1], pad], axis=0).T.astype(BF16)
    for q in range(2):
        right[0, q, main + faces :, :] = pad.astype(BF16)
    pl.semaphore_wait(barrier, len(peers))

    started = []

    def send(src, dst, s_sem, r_sem, to):
        copy = pltpu.make_async_remote_copy(
            src_ref=src, dst_ref=dst, send_sem=s_sem, recv_sem=r_sem, device_id=to, device_id_type=MESH
        )
        copy.start()
        started.append(copy)
        return copy

    def around(count, make):
        made = {d: make(d) for d in sorted(range(1, count), key=lambda d: -min(d, count - d))}
        return [made[d] for d in range(1, count)]

    copy_y = send(face, halo_y, halo_send.at[0], halo_recv.at[0], before_y)
    copies_x = [
        send(ev_in.at[:, :, zz, 0], halo_x.at[:, :, zz], halo_send.at[1 + zz], halo_recv.at[1 + zz], before_x)
        for zz in range(nz)
    ]

    copy_p = send(peram_in, peram.at[1], peram_send, peram_recv, sibling)

    def colour(h, columns, source, row_of):
        coef = [jnp.broadcast_to(column, (column.shape[0], LANES)) for column in columns]
        for lane in range(vecs // LANES):
            at = slice(lane * LANES, (lane + 1) * LANES)
            v = [[source(p, c, at) for c in range(3)] for p in range(2)]
            for a in range(3):
                re = im = None
                for b in range(3):
                    u_re, u_im = coef[a * 3 + b], coef[9 + a * 3 + b]
                    t_re = u_re * v[0][b] - u_im * v[1][b]
                    t_im = u_re * v[1][b] + u_im * v[0][b]
                    re = t_re if re is None else re + t_re
                    im = t_im if im is None else im + t_im
                re, im = re.astype(BF16), im.astype(BF16)
                right[h, 0, row_of(0, a), at] = re
                right[h, 0, row_of(1, a), at] = im
                right[h, 1, row_of(0, a), at] = im
                right[h, 1, row_of(1, a), at] = -re

    def plane_columns(h, zz, xx):
        columns = links[pl.ds((1 - h) * 18 * planes + zz * nx + xx, 18, stride=planes), :].T
        return [columns[:, i : i + 1] for i in range(18)]

    def plane_rows(zz, xx):
        def row_of(p, c):
            if xx < nx - 1:
                start = (((p * 3 + c) * nz + zz) * (nx - 1) + xx) * ny
            else:
                start = inner + ((p * 3 + c) * nz + zz) * ny
            return slice(start, start + ny) if isinstance(start, int) else pl.ds(pl.multiple_of(start, ny), ny)

        return row_of

    def hop_x_inner(zz, carry):
        for xx in range(nx - 1):
            colour(1, plane_columns(1, zz, xx), lambda p, c, at: ev[p, c, zz, xx + 1, :, at].astype(F32),
                   plane_rows(zz, xx))
        return carry

    def hop_x_last():
        for zz in range(nz):
            colour(1, plane_columns(1, zz, nx - 1), lambda p, c, at: halo_x[p, c, zz, :, at].astype(F32),
                   plane_rows(zz, nx - 1))

    def hop_y_main(zz, carry):
        last = lax.broadcasted_iota(jnp.int32, (ny, LANES), 0) == ny - 1
        for xx in range(nx):
            def source(p, c, at):
                return jnp.where(last, 0.0, pltpu.roll(ev[p, c, zz, xx, :, at].astype(F32), ny - 1, 0))

            colour(0, plane_columns(0, zz, xx), source, plane_rows(zz, xx))
        return carry

    def hop_y_edge():
        first_row = 18 * planes
        columns = [links[first_row + i * planes : first_row + (i + 1) * planes, ny - 1 : ny] for i in range(18)]

        def row_of(p, c):
            start = main + (p * 3 + c) * planes
            return slice(start, start + planes)

        def source(p, c, at):
            return halo_y[(p * 3 + c) * planes : (p * 3 + c + 1) * planes, at].astype(F32)

        colour(0, columns, source, row_of)

    def gram(h, q, low, high):
        lhs = vt[:, low:high]
        for j in range(vecs // (2 * LANES)):
            rhs = right[h, q, low:high, j * 2 * LANES : (j + 1) * 2 * LANES]
            value = jnp.dot(lhs, rhs, preferred_element_type=F32) * norm
            for half in range(2):
                yield slice((2 * j + half) * vecs, (2 * j + half + 1) * vecs), value[:, half * LANES : (half + 1) * LANES]

    def gram_x_inner():
        for at, value in gram(1, 1 - core, 0, inner):
            other[at, :] = value
        for at, value in gram(1, core, 0, inner):
            own[1, at, :] = value

    def to_core(h, s):
        mine = pl.ds(s * part, part)
        return send(send0.at[h, mine], recv0.at[h, mine], core_send.at[h, s], core_recv.at[h, s], sibling)

    def gram_x_other():
        copies = []
        for n, (at, value) in enumerate(gram(1, 1 - core, inner, main)):
            send0[1, at, :] = (other[at, :] + value).astype(BF16)
            if n % 2 == 1:
                copies.append(to_core(1, n // 2))
        return copies

    def gram_x_own():
        for at, value in gram(1, core, inner, main):
            own[1, at, :] += value

    def gram_y_other():
        copies = []
        for n, (at, value) in enumerate(gram(0, 1 - core, 0, vt.shape[1])):
            send0[0, at, :] = value.astype(BF16)
            if n % 2 == 1:
                copies.append(to_core(0, n // 2))
        return copies

    def gram_y_own():
        for at, value in gram(0, core, 0, vt.shape[1]):
            own[0, at, :] = value

    first = ((x, at_x), (y, at_y))
    second = ((y, at_y), (x, at_x))
    half = own.shape[1]
    part, len1, len2, len3 = half // 2, half // 8, half // 32, half // 256

    def start1(h, copies):
        result = []
        for s in range(2):
            copies[s].wait_recv()
            mine = pl.ds(s * part, part)
            total = own[h, mine] + recv0[h, mine].astype(F32)
            own[h, mine] = total
            send1[h, mine] = total.astype(BF16)
            result.append(around(4, lambda d: send(
                send1.at[h, pl.ds(s * part + (first[s][0] + d) % 4 * len1, len1)], recv1.at[h, s, d - 1],
                ring_send.at[h, 0, s, d - 1], ring_recv.at[h, 0, s, d - 1], first[s][1](d))))
        return result

    def start2(h, copies):
        result = []
        for s in range(2):
            total = own[h, pl.ds(s * part + first[s][0] * len1, len1)]
            for d, copy in enumerate(copies[s]):
                copy.wait_recv()
                total = total + recv1[h, s, d].astype(F32)
            own2[h, s] = total
            send2[h, s] = total.astype(BF16)
            place, at = second[s]
            result.append(around(4, lambda d: send(
                send2.at[h, s, pl.ds((place + d) % 4 * len2, len2)], recv2.at[h, s, d - 1],
                ring_send.at[h, 1, s, d - 1], ring_recv.at[h, 1, s, d - 1], at(d))))
        return result

    def start3(h, copies):
        totals = []
        for s in range(2):
            total = own2[h, s, pl.ds(second[s][0] * len2, len2)]
            for d, copy in enumerate(copies[s]):
                copy.wait_recv()
                total = total + recv2[h, s, d].astype(F32)
            totals.append(total)
        total = jnp.concatenate(
            [totals[s][i * len3 : (i + 1) * len3] for i in range(NZ_RING) for s in range(2)], axis=0
        )
        own3[h] = total
        send3[h] = total.astype(BF16)
        return around(NZ_RING, lambda d: send(
            send3.at[h, pl.ds((z + d) % NZ_RING * 2 * len3, 2 * len3)], recv3.at[h, d - 1],
            z_send.at[h, 0, d - 1], z_recv.at[h, 0, d - 1], at_z(d)))

    def base(s):
        b0 = s * part
        b1 = b0 + first[s][0] * len1
        return b0, b1, b1 + second[s][0] * len2

    def gather3(h, copies):
        place = pl.ds(z * 2 * len3, 2 * len3)
        total = own3[h, place]
        for d, copy in enumerate(copies):
            copy.wait_recv()
            total = total + recv3[h, d].astype(F32)
        done3[h, place] = total.astype(BF16)
        return around(NZ_RING, lambda d: send(
            done3.at[h, place], done3.at[h, place], z_send.at[h, 1, d - 1], z_recv.at[h, 1, d - 1], at_z(d)))

    def gather2(h, copies):
        for copy in copies:
            copy.wait_recv()
        value = done3[h].astype(F32)
        result = []
        for s in range(2):
            place = pl.ds(base(s)[2], len2)
            out[h, place] = jnp.concatenate(
                [value[(2 * i + s) * len3 : (2 * i + s + 1) * len3] for i in range(NZ_RING)], axis=0
            ).astype(BF16)
            result += around(4, lambda d: send(
                out.at[h, place], out.at[h, place], ring_send.at[h, 2, s, d - 1], ring_recv.at[h, 2, s, d - 1],
                second[s][1](d)))
        return result

    def gather1(h, copies):
        for copy in copies:
            copy.wait_recv()
        result = []
        for s in range(2):
            place = pl.ds(base(s)[1], len1)
            result += around(4, lambda d: send(
                out.at[h, place], out.at[h, place], ring_send.at[h, 3, s, d - 1], ring_recv.at[h, 3, s, d - 1],
                first[s][1](d)))
        return result

    m = lhs.shape[1] - vecs // n_gx
    own_rows = lhs.shape[1] - m

    def make_lhs():
        rows = peram.shape[2]
        for who in range(2):
            place = gx if who == 0 else gx + 1 - 2 * core
            for p in range(2):
                value = peram[who, p].astype(F32)
                for t in range(4):
                    start = (p * 4 + t) * rows
                    lhs_f[who, start : start + rows, :] = value[:, t * vecs : (t + 1) * vecs]
            column = lax.broadcasted_iota(jnp.int32, (own_rows, vecs), 1)
            row = lax.broadcasted_iota(jnp.int32, (own_rows, vecs), 0)
            lhs_f[who, m:, :] = jnp.where(column == place * own_rows + row, 1.0, 0.0)
        lhs[...] = lhs_f[...].astype(BF16)

    def contract(h, copies):
        for copy in copies:
            copy.wait_recv()
        blocks = out.shape[1] // vecs
        value = jnp.concatenate([out[h, j * vecs : (j + 1) * vecs, :] for j in range(blocks)], axis=1)
        across = (((1,), (1,)), ((), ()))
        there[h, 0] = jnp.dot(lhs[1], value, preferred_element_type=F32)
        there[h, 1] = lax.dot_general(lhs[1], value, across, preferred_element_type=F32)
        copy = send(there.at[h], products.at[core, h], core_send.at[h, 2], core_recv.at[h, 2], sibling)
        products[core, h, 0] = jnp.dot(lhs[0], value, preferred_element_type=F32)
        products[core, h, 1] = lax.dot_general(lhs[0], value, across, preferred_element_type=F32)
        return [copy]

    def combine(h, copies):
        copies[0].wait_recv()
        low = m // 2
        re, im = products[0, h, 0], products[1, h, 0]
        parts[h, 0] = (re[:low] - im[low:m]).astype(BF16)
        parts[h, 1] = (im[:low] + re[low:m]).astype(BF16)
        picks[h, 0] = re[m:]
        picks[h, 1] = im[m:]
        re, im = products[0, h, 1], products[1, h, 1]
        parts[2 + h, 0] = (re[:low] + im[low:m]).astype(BF16)
        parts[2 + h, 1] = (re[low:m] - im[:low]).astype(BF16)
        picks[2 + h, 0] = re[m:]
        picks[2 + h, 1] = -im[m:]

    loads[1].wait()
    for zz in range(nz):
        hop_x_inner(zz, 0)
    gram_x_inner()
    for zz in range(nz):
        hop_y_main(zz, 0)
    copy_y.wait_recv()
    hop_y_edge()
    b = gram_y_other()
    for copy in copies_x:
        copy.wait_recv()
    hop_x_last()
    a = gram_x_other()
    gram_y_own()
    b = start1(0, b)
    gram_x_own()
    a = start1(1, a)
    loads[2].wait()
    copy_p.wait_recv()
    make_lhs()
    for step in (start2, start3, gather3, gather2, gather1, contract):
        b = step(0, b)
        a = step(1, a)
    combine(0, b)
    combine(1, a)
    for copy in started:
        copy.wait_send()


def place_kernel(directions, spins, parts, picks, elementals, contracted):
    rows, vecs = contracted.shape[2], elementals.shape[3]
    for k in range(4):
        which = jnp.where(directions[k] % 2 == 0, directions[k] + 1, directions[k] - 1)
        elementals[k] = picks[which]
        for q in range(2):
            for u in range(4):
                contracted[k, q, :, u * vecs : (u + 1) * vecs] = parts[which, q, spins[u]]


def local(eigen_vecs, gauge_links, directions, spin_map, perambulator):
    reim, colours, nz, nx, ny, vecs = eigen_vecs.shape
    sites = nz * nx * ny * lax.axis_size("gx") * lax.axis_size("gy")
    norm = 1.0 / math.sqrt(3.0 * sites)
    ev = eigen_vecs
    links = gauge_links.reshape(-1, ny)
    half = vecs * vecs // LANES
    vmem = pl.BlockSpec(memory_space=pltpu.VMEM)
    faces = reim * colours * nz * nx
    summed = faces * ny + -(-faces // LANES) * LANES
    rows = perambulator.shape[1]
    own_rows = vecs // lax.axis_size("gx")
    lhs_rows = 8 * rows + own_rows
    parts, picks = pl.pallas_call(
        lambda *refs: reduce_kernel(norm, *refs),
        out_shape=(
            jax.ShapeDtypeStruct((4, 2, 4 * rows, vecs), BF16),
            jax.ShapeDtypeStruct((4, 2, own_rows, vecs), F32),
        ),
        in_specs=[pl.BlockSpec(memory_space=pltpu.HBM)] * 3,
        out_specs=(vmem, vmem),
        scratch_shapes=[
            pltpu.VMEM((2, 2, 2, lhs_rows, vecs), F32),
            pltpu.VMEM((2, half, LANES), BF16),
            pltpu.VMEM(ev.shape, BF16),
            pltpu.VMEM(links.shape, F32),
            pltpu.VMEM((2, *perambulator.shape), BF16),
            pltpu.VMEM((2, lhs_rows, vecs), F32),
            pltpu.VMEM((2, lhs_rows, vecs), BF16),
            pltpu.VMEM((vecs, summed), BF16),
            pltpu.VMEM((2, 2, summed, vecs), BF16),
            pltpu.VMEM((2, faces, vecs), F32),
            pltpu.VMEM((faces, vecs), BF16),
            pltpu.VMEM((faces, vecs), BF16),
            pltpu.VMEM((reim, colours, nz, ny, vecs), BF16),
            pltpu.VMEM((2, half, LANES), BF16),
            pltpu.VMEM((2, half, LANES), F32),
            pltpu.VMEM((half, LANES), F32),
            pltpu.VMEM((2, half, LANES), BF16),
            pltpu.VMEM((2, half, LANES), BF16),
            pltpu.VMEM((2, 2, 3, half // 8, LANES), BF16),
            pltpu.VMEM((2, 2, half // 8, LANES), F32),
            pltpu.VMEM((2, 2, half // 8, LANES), BF16),
            pltpu.VMEM((2, 2, 3, half // 32, LANES), BF16),
            pltpu.VMEM((2, half // 16, LANES), F32),
            pltpu.VMEM((2, half // 16, LANES), BF16),
            pltpu.VMEM((2, NZ_RING - 1, half // 128, LANES), BF16),
            pltpu.VMEM((2, half // 16, LANES), BF16),
            pltpu.VMEM((2, 2, lhs_rows, vecs), F32),
            pltpu.SemaphoreType.DMA((3,)),
            pltpu.SemaphoreType.DMA,
            pltpu.SemaphoreType.DMA,
            pltpu.SemaphoreType.DMA((1 + nz,)),
            pltpu.SemaphoreType.DMA((1 + nz,)),
            pltpu.SemaphoreType.DMA((2, 3)),
            pltpu.SemaphoreType.DMA((2, 3)),
            pltpu.SemaphoreType.DMA((2, 4, 2, 3)),
            pltpu.SemaphoreType.DMA((2, 4, 2, 3)),
            pltpu.SemaphoreType.DMA((2, 2, NZ_RING - 1)),
            pltpu.SemaphoreType.DMA((2, 2, NZ_RING - 1)),
        ],
        compiler_params=pltpu.CompilerParams(
            collective_id=0, has_side_effects=True, vmem_limit_bytes=int(53.35 * 2**20)
        ),
        name="reduce",
    )(ev, links, perambulator)
    smem = pl.BlockSpec(memory_space=pltpu.SMEM)
    return pl.pallas_call(
        place_kernel,
        out_shape=(
            jax.ShapeDtypeStruct((4, 2, own_rows, vecs), F32),
            jax.ShapeDtypeStruct((4, 2, rows, 4 * vecs), BF16),
        ),
        in_specs=[smem, smem, vmem, vmem],
        out_specs=(vmem, vmem),
        compiler_params=pltpu.CompilerParams(vmem_limit_bytes=32 * 2**20),
        name="place",
    )(directions, spin_map, parts.reshape(4, 2, 4, rows, vecs), picks)


def solution(mesh):
    in_specs = (
        P(None, None, None, "gx", "gy", None),
        P(None, None, None, None, None, "gx", "gy"),
        P(),
        P(),
        P(None, ("gx", "gy"), None),
    )
    out_specs = (P(None, None, "gx", None), P(None, None, ("gx", "gy"), None))
    return jax.shard_map(local, mesh=mesh, in_specs=in_specs, out_specs=out_specs, check_vma=False)
```
